32 devices in a mesh: context: 8 (over z, core), tensor: 4 (over y, x).
Axes of the slice: x: 2, y: 2, z: 4, core: 2. Of those that a mesh axis runs over, the one named last changes fastest.
Arguments:
- block_in: bfloat16 [8, 1024, 2048], P(None, 'context', 'tensor'), may hold values from -6 to 6
- norm_gain: bfloat16 [2048], P('tensor'), may hold values from 0.5 to 1.5
- layer_norm_bias: bfloat16 [2048], P('tensor'), may hold values from -2 to 2
- qkv_weight: bfloat16 [3, 2048, 2048], P(None, 'context', 'tensor'), may hold values from -0.125 to 0.125
- qkv_bias: bfloat16 [3, 2048], P(None, 'tensor'), may hold values from -3 to 3
- out_weight: bfloat16 [2048, 2048], P('tensor', 'context'), may hold values from -3 to 3
- out_bias: bfloat16 [2048], P('tensor'), may hold values from -2 to 2
- fc1_weight: bfloat16 [2048, 8192], P('context', 'tensor'), may hold values from -0.125 to 0.125
- fc1_bias: bfloat16 [8192], P('tensor'), may hold values from -3 to 3
- fc2_weight: bfloat16 [8192, 2048], P('tensor', 'context'), may hold values from -0.0625 to 0.0625
- fc2_bias: bfloat16 [2048], P('tensor'), may hold values from -2 to 2
- block_order: int32 [8], replicated, may hold values from 0 to 7, each once
- out_grad: bfloat16 [8, 1024, 2048], P(None, 'context', 'tensor'), may hold values from -6 to 6
Outputs:
- block_out: bfloat16 [8, 1024, 2048], P(None, 'context', 'tensor')
- input_grad: float32 [8, 1024, 2048], P(None, 'context', 'tensor')
- norm_gain_grad: float32 [2048], P('tensor')
- norm_bias_grad: float32 [2048], P('tensor')
- qkv_weight_grad: float32 [3, 2048, 2048], P(None, 'context', 'tensor')
- qkv_bias_grad: float32 [3, 2048], P(None, 'tensor')
- out_weight_grad: float32 [2048, 2048], P('tensor', 'context')
- out_bias_grad: float32 [2048], P('tensor')
- fc1_weight_grad: float32 [2048, 8192], P('context', 'tensor')
- fc1_bias_grad: float32 [8192], P('tensor')
- fc2_weight_grad: float32 [8192, 2048], P('tensor', 'context')
- fc2_bias_grad: float32 [2048], P('tensor')
The draws below stay inside these ranges and needn't reach their ends.
Inputs may be any that keep to these rules, and one draw needn't show every extreme that they name: Each index of context appears once; index c of context holds positions 128 * block_order[c] to 128 * block_order[c] + 127 of every sequence.
All inputs are finite; a program needn't handle non-finite values.
Results may differ from the reference program's by a relative error of at most 0.012.
Values may be sent and summed in bfloat16 or wider, within the bound.
No kernel may reach another device: no remote copies, remote signals or barrier semaphores. Data moves between devices by JAX's collectives and lax.ppermute only.
A program may use at most 320 MiB of HBM per device.

```python
import math
import jax
import jax.numpy as jnp
from jax import lax

D = 2048
HEADS = 32
HD = 64
ROT = 32
FF = 8192
SEQS = 8
LENGTH = 1024
N_CONTEXT = 8


def steps_of(own_key, extent, pieces, low, high):
    gain = 1.0
    for position, blocks in pieces:
        steps = jax.random.uniform(jax.random.fold_in(jax.random.fold_in(own_key, 6), position), (blocks,), jnp.float32, low / len(pieces), high / len(pieces))
        gain = gain * jnp.repeat(jnp.exp(steps), extent[position] // blocks).reshape((-1,) + (1,) * (len(extent) - 1 - position))
    return gain


def bell_draw(stream_key, shape, width, reach, shards=(), kind=jnp.bfloat16):
    entries = jax.random.normal(stream_key, shape, jnp.float32) * width
    if len(shards) > 0:
        entries = steps_of(stream_key, shape, shards, -0.22, 0.18) * entries
    return jnp.clip(entries, min=-reach, max=reach).astype(kind)


def setup_inputs(seed: int = 0) -> dict:
    splits = jax.random.split(jax.random.key(seed), 14)
    return {
        "block_in": bell_draw(splits[0], (SEQS, LENGTH, D), 1.0, 6.0, ((1, 8), (2, 4))),
        "norm_gain": jnp.clip(1.0 + 0.1 * jax.random.normal(splits[1], (D,), jnp.float32), 0.5, 1.5).astype(jnp.bfloat16),
        "layer_norm_bias": bell_draw(splits[2], (D,), 0.3, 2.0, ((0, 4),)),
        "qkv_weight": bell_draw(splits[3], (3, D, D), D ** -0.5, 0.125, ((1, 8), (2, 4))),
        "qkv_bias": bell_draw(splits[4], (3, D), 0.5, 3.0, ((1, 4),)),
        "out_weight": bell_draw(splits[5], (D, D), 4 ** -0.5, 3.0, ((0, 4), (1, 8))),
        "out_bias": bell_draw(splits[6], (D,), 0.3, 2.0, ((0, 4),)),
        "fc1_weight": bell_draw(splits[7], (D, FF), D ** -0.5, 0.125, ((0, 8), (1, 4))),
        "fc1_bias": bell_draw(splits[8], (FF,), 0.5, 3.0, ((0, 4),)),
        "fc2_weight": bell_draw(splits[9], (FF, D), FF ** -0.5, 0.0625, ((0, 4), (1, 8))),
        "fc2_bias": bell_draw(splits[10], (D,), 0.3, 2.0, ((0, 4),)),
        "block_order": jax.random.permutation(splits[11], N_CONTEXT).astype(jnp.int32),
        "out_grad": bell_draw(splits[12], (SEQS, LENGTH, D), 1.0, 6.0, ((1, 8), (2, 4))),
    }


NORM_EPS = 1e-05
NEG_BIG = -1e+30
GELU_COEF = 0.7978845608028654

def gelu_tanh(values):
    return 0.5 * values * (1.0 + jnp.tanh(GELU_COEF * (values + 0.044715 * values * values * values)))

def norm_pieces_list(row_group):
    mean_row = lax.optimization_barrier(jnp.mean(row_group, -1, keepdims=True))
    centred = row_group - mean_row
    spread = lax.optimization_barrier(jnp.mean(centred * centred, -1, keepdims=True))
    inverse_deviation = lax.rsqrt(spread + NORM_EPS)
    return (centred * inverse_deviation, inverse_deviation)

def angle_tables(positions):
    half_rot = ROT // 2
    freqs = jnp.exp(jnp.arange(half_rot, dtype=jnp.float32) * (-2.0 * math.log(10000.0) / ROT))
    angles = positions.astype(jnp.float32)[:, None] * freqs[None, :]
    cosine = jnp.cos(angles)
    sine = jnp.sin(angles)
    return (jnp.concatenate([cosine, cosine], -1), jnp.concatenate([sine, sine], -1))

def rotate_fwd(values, cosine, sine):
    half_rot = ROT // 2
    front = values[..., :ROT]
    turned = jnp.concatenate([-front[..., half_rot:], front[..., :half_rot]], -1)
    return jnp.concatenate([front * cosine + turned * sine, values[..., ROT:]], -1)

def rotate_back(grads, cosine, sine):
    half_rot = ROT // 2
    front = grads[..., :ROT]
    by_sine = front * sine
    turned = jnp.concatenate([by_sine[..., half_rot:], -by_sine[..., :half_rot]], -1)
    return jnp.concatenate([front * cosine + turned, grads[..., ROT:]], -1)

def reference(block_in, norm_gain, layer_norm_bias, qkv_weight, qkv_bias, out_weight, out_bias, fc1_weight, fc1_bias, fc2_weight, fc2_bias, block_order, out_grad):
    seq_len = block_in.shape[1]
    block_len = seq_len // N_CONTEXT
    positions = (block_order[:, None] * block_len + jnp.arange(block_len, dtype=jnp.int32)[None, :]).reshape(seq_len).astype(jnp.int32)
    cosine, sine = angle_tables(positions)
    cos3 = cosine[:, None, :]
    sin3 = sine[:, None, :]
    causal = positions[None, :] <= positions[:, None]
    scale_qk = HD ** (-0.5)
    gain_single_precision = norm_gain.astype(jnp.float32)

    def head_forward(items):
        query_h, key_h, value_h = items
        scores = jnp.dot(query_h, key_h.T, preferred_element_type=jnp.float32) * scale_qk
        scores = jnp.where(causal, scores, NEG_BIG)
        row_max = lax.optimization_barrier(jnp.max(scores, -1))
        weights = jnp.where(causal, jnp.exp(scores - row_max[:, None]), 0.0)
        row_sum = lax.optimization_barrier(jnp.sum(weights, -1))
        mixed = jnp.dot(weights.astype(jnp.bfloat16), value_h, preferred_element_type=jnp.float32) / row_sum[:, None]
        return (mixed, row_max + jnp.log(row_sum))

    def head_backward(items):
        query_h, key_h, value_h, attn_h, grad_h, total_h = items
        scores = jnp.dot(query_h, key_h.T, preferred_element_type=jnp.float32) * scale_qk
        probs = jnp.where(causal, jnp.exp(scores - total_h[:, None]), 0.0)
        value_grad = jnp.dot(probs.astype(jnp.bfloat16).T, grad_h, preferred_element_type=jnp.float32)
        prob_grad = jnp.dot(grad_h, value_h.T, preferred_element_type=jnp.float32)
        delta = lax.optimization_barrier(jnp.sum(grad_h.astype(jnp.float32) * attn_h.astype(jnp.float32), -1))
        score_grad = (probs * (prob_grad - delta[:, None]) * scale_qk).astype(jnp.bfloat16)
        query_grad = jnp.dot(score_grad, key_h, preferred_element_type=jnp.float32)
        key_grad = jnp.dot(score_grad.T, query_h, preferred_element_type=jnp.float32)
        return (query_grad, key_grad, value_grad)

    def to_heads(values):
        return values.reshape(seq_len, HEADS, HD).transpose(1, 0, 2)

    def from_heads(values):
        return values.transpose(1, 0, 2).reshape(seq_len, D)

    def one_sequence(totals, items):
        row_group, grads = items
        centred_scaled, inverse_deviation = norm_pieces_list(row_group.astype(jnp.float32))
        normalised_rows = (centred_scaled * gain_single_precision + layer_norm_bias.astype(jnp.float32)).astype(jnp.bfloat16)
        proj = [jnp.dot(normalised_rows, qkv_weight[j], preferred_element_type=jnp.float32) + qkv_bias[j].astype(jnp.float32) for j in range(3)]
        queries = rotate_fwd(proj[0].reshape(seq_len, HEADS, HD), cos3, sin3).reshape(seq_len, D).astype(jnp.bfloat16)
        keys_rot = rotate_fwd(proj[1].reshape(seq_len, HEADS, HD), cos3, sin3).reshape(seq_len, D).astype(jnp.bfloat16)
        values_b = proj[2].astype(jnp.bfloat16)
        mixed, log_total = lax.map(head_forward, (to_heads(queries), to_heads(keys_rot), to_heads(values_b)))
        attn = from_heads(mixed).astype(jnp.bfloat16)
        attn_part = jnp.dot(attn, out_weight, preferred_element_type=jnp.float32)
        hidden_pre = jnp.dot(normalised_rows, fc1_weight, preferred_element_type=jnp.float32) + fc1_bias.astype(jnp.float32)
        hidden_act = gelu_tanh(hidden_pre).astype(jnp.bfloat16)
        mlp_part = jnp.dot(hidden_act, fc2_weight, preferred_element_type=jnp.float32)
        out_rows = (row_group.astype(jnp.float32) + attn_part + mlp_part + out_bias.astype(jnp.float32) + fc2_bias.astype(jnp.float32)).astype(jnp.bfloat16)
        gradient_single_precision = grads.astype(jnp.float32)
        outb_sum = lax.optimization_barrier(jnp.sum(gradient_single_precision, 0))
        outw_grad = jnp.dot(attn.T, grads, preferred_element_type=jnp.float32)
        fc2_grad = jnp.dot(hidden_act.T, grads, preferred_element_type=jnp.float32)
        attn_grad = jnp.dot(grads, out_weight.T, preferred_element_type=jnp.float32).astype(jnp.bfloat16)
        act_grad = jnp.dot(grads, fc2_weight.T, preferred_element_type=jnp.float32)
        _, pullback = jax.vjp(gelu_tanh, hidden_pre)
        hidden_grad = pullback(act_grad)[0]
        hidden_grad_b = hidden_grad.astype(jnp.bfloat16)
        fc1_grad = jnp.dot(normalised_rows.T, hidden_grad_b, preferred_element_type=jnp.float32)
        fc1b_sum = lax.optimization_barrier(jnp.sum(hidden_grad, 0))
        query_grad, key_grad, value_grad = lax.map(head_backward, (to_heads(queries), to_heads(keys_rot), to_heads(values_b), to_heads(attn), to_heads(attn_grad), log_total))
        query_pre = rotate_back(from_heads(query_grad).reshape(seq_len, HEADS, HD), cos3, sin3).reshape(seq_len, D)
        key_pre = rotate_back(from_heads(key_grad).reshape(seq_len, HEADS, HD), cos3, sin3).reshape(seq_len, D)
        proj_grad = jnp.stack([query_pre, key_pre, from_heads(value_grad)])
        qkvb_sum = lax.optimization_barrier(jnp.sum(proj_grad, 1))
        proj_grad_b = proj_grad.astype(jnp.bfloat16)
        qkv_grad = jnp.stack([jnp.dot(normalised_rows.T, proj_grad_b[j], preferred_element_type=jnp.float32) for j in range(3)])
        norm_output_grad = jnp.dot(hidden_grad_b, fc1_weight.T, preferred_element_type=jnp.float32)
        for j in range(3):
            norm_output_grad = norm_output_grad + jnp.dot(proj_grad_b[j], qkv_weight[j].T, preferred_element_type=jnp.float32)
        gain_total_grad = lax.optimization_barrier(jnp.sum(norm_output_grad * centred_scaled, 0))
        beta_sum = lax.optimization_barrier(jnp.sum(norm_output_grad, 0))
        scaled_rows = norm_output_grad * gain_single_precision
        input_row_block = gradient_single_precision + inverse_deviation * (scaled_rows - lax.optimization_barrier(jnp.mean(scaled_rows, -1, keepdims=True)) - centred_scaled * lax.optimization_barrier(jnp.mean(scaled_rows * centred_scaled, -1, keepdims=True)))
        adds = (gain_total_grad, beta_sum, qkv_grad, qkvb_sum, outw_grad, outb_sum, fc1_grad, fc1b_sum, fc2_grad)
        totals = tuple((a + b for a, b in zip(totals, adds)))
        return (totals, (out_rows, input_row_block))
    start = (jnp.zeros((D,), jnp.float32), jnp.zeros((D,), jnp.float32), jnp.zeros((3, D, D), jnp.float32), jnp.zeros((3, D), jnp.float32), jnp.zeros((D, D), jnp.float32), jnp.zeros((D,), jnp.float32), jnp.zeros((D, FF), jnp.float32), jnp.zeros((FF,), jnp.float32), jnp.zeros((FF, D), jnp.float32))
    totals, (block_out, input_grad) = lax.scan(one_sequence, start, (block_in, out_grad))
    gain_g, beta_g, qkv_w_g, qkv_b_g, outw_g, outb_g, fc1_w_g, fc1_b_g, fc2_w_g = totals
    return (block_out, input_grad, gain_g, beta_g, qkv_w_g, qkv_b_g, outw_g, outb_g, fc1_w_g, fc1_b_g, fc2_w_g, outb_g)
```

```python
import functools
import math

import jax
import jax.numpy as jnp
from jax import lax
from jax.experimental import pallas as pl
from jax.experimental.pallas import tpu as pltpu
from jax.sharding import PartitionSpec as P

HD = 64
ROT = 32

NORM_EPS = 1e-05
NEG_BIG = -1e30
GELU_COEF = 0.7978845608028654
GELU_CUBE = 0.044715

f32 = jnp.float32
bf16 = jnp.bfloat16


def dot(spec, a, b):
    return jnp.einsum(spec, a, b, preferred_element_type=f32)


def gelu_and_slope(h):
    t = jnp.tanh(GELU_COEF * (h + GELU_CUBE * h * h * h))
    act = 0.5 * h * (1.0 + t)
    slope = 0.5 * (1.0 + t) + 0.5 * h * (1.0 - t * t) * GELU_COEF * (
        1.0 + 3.0 * GELU_CUBE * h * h
    )
    return act, slope


def swap(value, axis, mask):
    size = lax.axis_size(axis)
    return lax.ppermute(value, axis, [(i, i ^ mask) for i in range(size)])


def sum_over(value, axis):
    size = lax.axis_size(axis)
    if size & (size - 1):
        return lax.psum(value, axis)
    mask = 1
    while mask < size:
        value = value + swap(value, axis, mask)
        mask *= 2
    return value


class Rows:
    def __init__(self, seq_count, block_order):
        self.n_ctx = lax.axis_size("context")
        self.members = math.gcd(seq_count, self.n_ctx)
        self.groups = self.n_ctx // self.members
        self.per = seq_count // self.members
        ctx = lax.axis_index("context")
        self.me = ctx % self.members
        start = ctx - self.me
        self.order = lax.dynamic_slice_in_dim(block_order, start, self.members)
        self.rank = jnp.sum(
            (self.order[None, :] < self.order[:, None]).astype(jnp.int32), axis=1
        )

    def _peer(self, step):
        if self.members & (self.members - 1):
            to = (self.me + step) % self.members
            fro = (self.me - step) % self.members
            table = [
                (i, i - i % self.members + (i + step) % self.members) for i in range(self.n_ctx)
            ]
        else:
            to = fro = self.me ^ step
            table = [(i, i ^ step) for i in range(self.n_ctx)]
        return to, fro, table

    def gather(self, rows):
        seqs, block, width = rows.shape
        split = rows.reshape(self.members, self.per, block, width)
        held = jnp.zeros((self.per, self.members, block, width), rows.dtype)
        for step in range(self.members):
            to, fro, table = self._peer(step)
            part = lax.dynamic_index_in_dim(split, to, 0, keepdims=False)
            if step:
                part = lax.ppermute(part, "context", table)
            held = lax.dynamic_update_slice(held, part[:, None], (0, self.rank[fro], 0, 0))
        return held.reshape(self.per * self.members * block, width)

    def scatter(self, rows):
        width = rows.shape[-1]
        split = rows.reshape(self.per, self.members, -1, width)
        block = split.shape[2]
        held = jnp.zeros((self.members, self.per, block, width), rows.dtype)
        for step in range(self.members):
            to, fro, table = self._peer(step)
            part = lax.dynamic_index_in_dim(split, self.rank[to], 1, keepdims=False)
            if step:
                part = lax.ppermute(part, "context", table)
            held = lax.dynamic_update_slice(held, part[None], (fro, 0, 0, 0))
        return held.reshape(self.members * self.per, block, width)


def gather_features(rows):
    if lax.axis_size("tensor") != 4:
        return lax.all_gather(rows, "tensor", axis=1, tiled=True)
    ten = lax.axis_index("tensor")
    count, width = rows.shape
    half = count // 2
    near_x = swap(rows, "tensor", 1)
    near_y = swap(rows, "tensor", 2)
    far_top = swap(near_y[:half], "tensor", 1)
    far_low = swap(near_x[half:], "tensor", 2)
    held = jnp.zeros((count, 4 * width), rows.dtype)
    for row, mask, part in (
        (0, 0, rows),
        (0, 1, near_x),
        (0, 2, near_y),
        (0, 3, far_top),
        (half, 3, far_low),
    ):
        held = lax.dynamic_update_slice(held, part, (row, (ten ^ mask) * width))
    return held


def sum_features(rows, width):
    if lax.axis_size("tensor") != 4:
        return lax.psum_scatter(
            rows.astype(bf16), "tensor", scatter_dimension=1, tiled=True
        ).astype(f32)
    ten = lax.axis_index("tensor")
    half = rows.shape[0] // 2

    def chunk(mask):
        return lax.dynamic_slice_in_dim(rows, (ten ^ mask) * width, width, 1).astype(f32)

    far = chunk(3).astype(bf16)
    via_x = swap(far[:half], "tensor", 1).astype(f32)
    via_y = swap(far[half:], "tensor", 2).astype(f32)
    to_y = chunk(2)
    to_y = jnp.concatenate([to_y[:half] + via_x, to_y[half:]], 0).astype(bf16)
    to_x = chunk(1)
    to_x = jnp.concatenate([to_x[:half], to_x[half:] + via_y], 0).astype(bf16)
    from_y = swap(to_y, "tensor", 2).astype(f32)
    from_x = swap(to_x, "tensor", 1).astype(f32)
    return chunk(0) + from_x + from_y


def sum_weight_rows(grads, axis):
    n_ctx = lax.axis_size("context")
    chain = n_ctx // 2
    ctx = lax.axis_index("context")
    z, k = ctx // 2, ctx % 2
    shape = grads.shape
    split = grads.reshape(shape[:axis] + (chain, 2, shape[axis] // n_ctx) + shape[axis + 1 :])
    mine = lax.dynamic_index_in_dim(split, k, axis + 1, keepdims=False)
    other = lax.dynamic_index_in_dim(split, 1 - k, axis + 1, keepdims=False)
    other = swap(other, "context", 1)

    def part(index):
        index = jnp.clip(index, 0, chain - 1)
        return lax.dynamic_index_in_dim(mine, index, axis, keepdims=False).astype(
            f32
        ) + lax.dynamic_index_in_dim(other, index, axis, keepdims=False).astype(f32)

    up = down = 0.0
    for step in range(1, chain):
        send = (part(chain - step + z) + up).astype(bf16)
        table = [(2 * i + c, 2 * i + 2 + c) for i in range(step) for c in range(2)]
        up = lax.ppermute(send, "context", table).astype(f32)
        send = (part(z - chain + step) + down).astype(bf16)
        table = [
            (2 * i + c, 2 * i - 2 + c) for i in range(chain - step, chain) for c in range(2)
        ]
        down = lax.ppermute(send, "context", table).astype(f32)
    return part(z) + up + down


def rotary_tables(length, lanes):
    half_rot = ROT // 2
    freqs = jnp.exp(jnp.arange(half_rot, dtype=f32) * (-2.0 * math.log(10000.0) / ROT))
    angles = jnp.arange(length, dtype=jnp.int32).astype(f32)[:, None] * freqs[None, :]
    cosine = jnp.cos(angles)
    sine = jnp.sin(angles)
    zero = jnp.zeros((length, half_rot), f32)
    rest_one = jnp.ones((length, HD - ROT), f32)
    rest_zero = jnp.zeros((length, HD - ROT), f32)
    keep = jnp.concatenate([cosine, cosine, rest_one], -1)
    from_high = jnp.concatenate([-sine, zero, rest_zero], -1)
    from_low = jnp.concatenate([zero, sine, rest_zero], -1)
    many = lanes // HD
    return jnp.stack([jnp.tile(v, (1, many)) for v in (keep, from_high, from_low)])


LANES = 128


def attention_kernel(tile, proj_ref, grad_ref, table_ref, attn_ref, dproj_ref, bias_ref, *scratch):
    q_s, k_s, v_s, g_s, qt_s, kt_s, vt_s, gt_s, at_s, dqt_s, dk_s, dv_s = scratch
    length = proj_ref.shape[1]
    tiles = length // tile
    half_rot = ROT // 2
    scale = HD ** (-0.5)
    many = LANES // HD

    def turn(u, sign):
        keep, high, low = table_ref[0], table_ref[1], table_ref[2]
        moved = pltpu.roll(u, LANES - half_rot, 1) * high + pltpu.roll(u, half_rot, 1) * low
        return u * keep + sign * moved

    q = turn(proj_ref[0], 1.0).astype(bf16).astype(f32) * scale
    k = turn(proj_ref[1], 1.0).astype(bf16).astype(f32)
    v = proj_ref[2].astype(bf16).astype(f32)
    g = grad_ref[...].astype(f32)
    for value, flat, turned in ((q, q_s, qt_s), (k, k_s, kt_s), (v, v_s, vt_s), (g, g_s, gt_s)):
        turned[...] = value.T.astype(bf16)
        for h in range(many):
            flat[h] = value[:, h * HD : (h + 1) * HD].astype(bf16)

    row = lax.broadcasted_iota(jnp.int32, (tile, tile), 0)
    col = lax.broadcasted_iota(jnp.int32, (tile, tile), 1)
    hidden = row > col

    def mm(a, b):
        return jnp.dot(a, b, preferred_element_type=f32)

    for h in range(many):
        feats = slice(h * HD, (h + 1) * HD)
        for i in range(tiles):
            qs = slice(i * tile, (i + 1) * tile)
            q_t = qt_s[feats, qs]
            scores = []
            for j in range(i + 1):
                s = mm(k_s[h, j * tile : (j + 1) * tile, :], q_t)
                scores.append(jnp.where(hidden, NEG_BIG, s) if j == i else s)
            top = functools.reduce(
                jnp.maximum, [jnp.max(s, axis=0, keepdims=True) for s in scores]
            )
            weights = [jnp.exp(s - top) for s in scores]
            total = functools.reduce(
                jnp.add, [jnp.sum(w, axis=0, keepdims=True) for w in weights]
            )
            mixed = functools.reduce(
                jnp.add,
                [
                    mm(vt_s[feats, j * tile : (j + 1) * tile], w.astype(bf16))
                    for j, w in enumerate(weights)
                ],
            )
            mixed = (mixed / total).astype(bf16).astype(f32)
            at_s[feats, qs] = mixed
            g_t = gt_s[feats, qs]
            delta = jnp.sum(g_t.astype(f32) * mixed, axis=0, keepdims=True)
            inverse = 1.0 / total
            dq = None
            for j in range(i + 1):
                ks = slice(j * tile, (j + 1) * tile)
                p = weights[j] * inverse
                dp = mm(v_s[h, ks, :], g_t)
                ds = (p * (dp - delta)).astype(bf16)
                dv = mm(p.astype(bf16), g_s[h, qs, :])
                dk = mm(ds, q_s[h, qs, :])
                if i == j:
                    dv_s[h, ks, :] = dv
                    dk_s[h, ks, :] = dk
                else:
                    dv_s[h, ks, :] += dv
                    dk_s[h, ks, :] += dk
                part = mm(kt_s[feats, ks], ds)
                dq = part if dq is None else dq + part
            dqt_s[feats, qs] = dq * scale

    attn_ref[...] = at_s[...].T.astype(bf16)
    dq = turn(dqt_s[...].T, -1.0)
    dk = turn(jnp.concatenate([dk_s[h] for h in range(many)], 1), -1.0)
    dv = jnp.concatenate([dv_s[h] for h in range(many)], 1)
    for index, value in enumerate((dq, dk, dv)):
        dproj_ref[index] = value.astype(bf16)
        bias_ref[0, index] = jnp.sum(value, axis=0, keepdims=True)


def attention_whole(proj, attn_grad, per):
    _, rows, width = proj.shape
    length = rows // per
    tile = min(256, length)
    many = LANES // HD
    tables = rotary_tables(length, LANES)
    flat = pltpu.VMEM((many, length, HD), bf16)
    turned = pltpu.VMEM((LANES, length), bf16)
    wide = pltpu.VMEM((LANES, length), f32)
    sums = pltpu.VMEM((many, length, HD), f32)
    attn, dproj, bias = pl.pallas_call(
        functools.partial(attention_kernel, tile),
        grid=(per, width // LANES),
        in_specs=[
            pl.BlockSpec((3, length, LANES), lambda s, h: (0, s, h)),
            pl.BlockSpec((length, LANES), lambda s, h: (s, h)),
            pl.BlockSpec((3, length, LANES), lambda s, h: (0, 0, 0)),
        ],
        out_specs=[
            pl.BlockSpec((length, LANES), lambda s, h: (s, h)),
            pl.BlockSpec((3, length, LANES), lambda s, h: (0, s, h)),
            pl.BlockSpec((1, 3, 1, LANES), lambda s, h: (s, 0, 0, h)),
        ],
        out_shape=[
            jax.ShapeDtypeStruct((rows, width), bf16),
            jax.ShapeDtypeStruct((3, rows, width), bf16),
            jax.ShapeDtypeStruct((per, 3, 1, width), f32),
        ],
        scratch_shapes=[flat] * 4 + [turned] * 4 + [wide] * 2 + [sums] * 2,
        compiler_params=pltpu.CompilerParams(vmem_limit_bytes=40 * 1024 * 1024),
        cost_estimate=pl.CostEstimate(
            flops=40 * rows * length * width,
            bytes_accessed=3 * rows * width * 6 + rows * width * 4,
            transcendentals=rows * length * width // HD,
        ),
    )(proj, attn_grad, tables)
    return attn, dproj, jnp.sum(bias, axis=(0, 2))


def rotate(values, cosine, sine):
    half_rot = ROT // 2
    front = values[..., :ROT]
    turned = jnp.concatenate([-front[..., half_rot:], front[..., :half_rot]], -1)
    return jnp.concatenate([front * cosine + turned * sine, values[..., ROT:]], -1)


def rotate_back(grads, cosine, sine):
    half_rot = ROT // 2
    front = grads[..., :ROT]
    by_sine = front * sine
    turned = jnp.concatenate([by_sine[..., half_rot:], -by_sine[..., :half_rot]], -1)
    return jnp.concatenate([front * cosine + turned, grads[..., ROT:]], -1)


def attention_split(proj, attn_grad, plan, block_len):
    _, rows, width = proj.shape
    per, members, groups = plan.per, plan.members, plan.groups
    count = rows // per
    heads = width // HD
    blocks = jnp.sum(
        jnp.where(
            plan.rank[None, :] == jnp.arange(members, dtype=jnp.int32)[:, None],
            plan.order[None, :],
            0,
        ),
        axis=1,
    )
    position = (
        blocks[:, None] * block_len + jnp.arange(block_len, dtype=jnp.int32)[None, :]
    ).reshape(count)
    half_rot = ROT // 2
    freqs = jnp.exp(jnp.arange(half_rot, dtype=f32) * (-2.0 * math.log(10000.0) / ROT))
    angles = position.astype(f32)[:, None] * freqs[None, :]
    cosine = jnp.concatenate([jnp.cos(angles)] * 2, -1)[None, :, None, :]
    sine = jnp.concatenate([jnp.sin(angles)] * 2, -1)[None, :, None, :]
    teams = [[m + members * g for g in range(groups)] for m in range(members)]

    def team_gather(value, axis):
        return lax.all_gather(
            value, "context", axis=axis, tiled=True, axis_index_groups=teams
        )

    def team_sum(value):
        return lax.psum_scatter(
            value, "context", scatter_dimension=1, tiled=True, axis_index_groups=teams
        )

    shape = (per, count, heads, HD)
    q = rotate(proj[0].reshape(shape), cosine, sine).astype(bf16)
    k = rotate(proj[1].reshape(shape), cosine, sine).astype(bf16)
    v = proj[2].reshape(shape).astype(bf16)
    g = attn_grad.reshape(shape)
    k_all = team_gather(k, 1)
    v_all = team_gather(v, 1)
    every = block_order_blocks(plan, teams, position)
    visible = every[None, :] <= position[:, None]
    scale = HD ** (-0.5)
    outs, dqs, dks, dvs = [], [], [], []
    for h in range(heads):
        s = dot("sqd,skd->sqk", q[:, :, h], k_all[:, :, h]) * scale
        s = jnp.where(visible, s, NEG_BIG)
        top = jnp.max(s, -1, keepdims=True)
        e = jnp.where(visible, jnp.exp(s - top), 0.0)
        total = jnp.sum(e, -1, keepdims=True)
        o = (dot("sqk,skd->sqd", e.astype(bf16), v_all[:, :, h]) / total).astype(bf16)
        delta = jnp.sum(g[:, :, h].astype(f32) * o.astype(f32), -1, keepdims=True)
        p = e / total
        dp = dot("sqd,skd->sqk", g[:, :, h], v_all[:, :, h])
        ds = (p * (dp - delta) * scale).astype(bf16)
        outs.append(o)
        dqs.append(dot("sqk,skd->sqd", ds, k_all[:, :, h]))
        dks.append(dot("sqk,sqd->skd", ds, q[:, :, h]))
        dvs.append(dot("sqk,sqd->skd", p.astype(bf16), g[:, :, h]))
    attn = jnp.concatenate(outs, -1).reshape(rows, width)
    dq = rotate_back(jnp.stack(dqs, 2), cosine, sine).reshape(rows, width)
    dk = team_sum(jnp.concatenate(dks, -1)).reshape(shape)
    dk = rotate_back(dk, cosine, sine).reshape(rows, width)
    dv = team_sum(jnp.concatenate(dvs, -1)).reshape(rows, width)
    dproj = jnp.stack([dq, dk, dv])
    return attn, dproj.astype(bf16), jnp.sum(dproj, axis=1)


def block_order_blocks(plan, teams, position):
    members, groups = plan.members, plan.groups
    order = plan.all_order.reshape(groups, members)
    blocks = jnp.sort(order, axis=1).reshape(-1)
    block_len = position.shape[0] // members
    return (
        blocks[:, None] * block_len + jnp.arange(block_len, dtype=jnp.int32)[None, :]
    ).reshape(-1)


def on_device(
    block_in,
    norm_gain,
    layer_norm_bias,
    qkv_weight,
    qkv_bias,
    out_weight,
    out_bias,
    fc1_weight,
    fc1_bias,
    fc2_weight,
    fc2_bias,
    block_order,
    out_grad,
):
    seq_count, block_len, width = block_in.shape
    plan = Rows(seq_count, block_order)
    plan.all_order = block_order
    ten = lax.axis_index("tensor")

    x_own = plan.gather(block_in)
    g_own = plan.gather(out_grad)
    x_own, qkv_weight, out_weight, fc1_weight, fc2_weight = lax.optimization_barrier(
        (x_own, qkv_weight, out_weight, fc1_weight, fc2_weight)
    )
    qkv_full = lax.all_gather(qkv_weight, "context", axis=1, tiled=True)
    out_full = lax.all_gather(out_weight, "context", axis=1, tiled=True)
    fc1_full = lax.all_gather(fc1_weight, "context", axis=0, tiled=True)
    fc2_full = lax.all_gather(fc2_weight, "context", axis=1, tiled=True)
    norm_both = gather_features(jnp.stack([norm_gain, layer_norm_bias]))
    x_full = gather_features(x_own)
    g_full = gather_features(g_own)

    gain = norm_both[0].astype(f32)
    shift = norm_both[1].astype(f32)
    x_single = x_full.astype(f32)
    mean = jnp.mean(x_single, -1, keepdims=True)
    centred = x_single - mean
    inv_std = lax.rsqrt(jnp.mean(centred * centred, -1, keepdims=True) + NORM_EPS)
    xhat = centred * inv_std
    normed = (xhat * gain + shift).astype(bf16)

    proj = dot("rd,jde->jre", normed, qkv_full) + qkv_bias.astype(f32)[:, None, :]
    attn_grad = dot("rd,ed->re", g_full, out_full).astype(bf16)
    if plan.groups == 1:
        attn, dproj, qkvb_sum = attention_whole(proj, attn_grad, plan.per)
    else:
        attn, dproj, qkvb_sum = attention_split(proj, attn_grad, plan, block_len)
    qkv_part = dot("rd,jre->jde", normed, dproj).astype(bf16)
    out_part = dot("rd,re->de", g_full, attn).astype(bf16)
    qkv_w_g = sum_weight_rows(qkv_part, 1)
    out_w_g = sum_weight_rows(out_part, 0).T

    hidden_pre = dot("rd,df->rf", normed, fc1_full) + fc1_bias.astype(f32)
    hidden_act, slope = gelu_and_slope(hidden_pre)
    hidden_act = hidden_act.astype(bf16)
    fc2_part = dot("rd,rf->df", g_full, hidden_act).astype(bf16)
    fc2_w_g = sum_weight_rows(fc2_part, 0).T
    act_grad = dot("rd,fd->rf", g_full, fc2_full)
    hidden_grad = act_grad * slope
    fc1b_sum = jnp.sum(hidden_grad, axis=0)
    hidden_grad = hidden_grad.astype(bf16)
    fc1_part = dot("rd,rf->df", normed, hidden_grad).astype(bf16)
    fc1_w_g = sum_weight_rows(fc1_part, 0)

    norm_part = dot("jre,jde->rd", dproj, qkv_full) + dot("rf,df->rd", hidden_grad, fc1_full)
    scaled = norm_part * gain
    row_sums = jnp.stack([jnp.sum(scaled, -1), jnp.sum(scaled * xhat, -1)])
    row_sums = sum_over(row_sums, "tensor") / x_full.shape[1]
    norm_own = sum_features(norm_part, width)
    xhat_own = (x_own.astype(f32) - mean) * inv_std
    gain_sum = jnp.sum(norm_own * xhat_own, axis=0)
    beta_sum = jnp.sum(norm_own, axis=0)
    change = inv_std * (
        norm_own * norm_gain.astype(f32)
        - row_sums[0][:, None]
        - xhat_own * row_sums[1][:, None]
    )
    grad_own = out_grad.astype(f32)
    input_grad = grad_own + plan.scatter(change.astype(bf16)).astype(f32)

    branch = dot("re,ed->rd", attn, out_full) + dot("rf,fd->rd", hidden_act, fc2_full)
    branch = plan.scatter(sum_features(branch, width).astype(bf16))
    block_out = (
        block_in.astype(f32)
        + branch.astype(f32)
        + out_bias.astype(f32)
        + fc2_bias.astype(f32)
    ).astype(bf16)

    outb_sum = jnp.sum(grad_own, axis=(0, 1))
    sums = (qkvb_sum.reshape(-1), outb_sum, fc1b_sum, gain_sum, beta_sum)
    joined = sum_over(jnp.concatenate(sums), "context")
    cuts = []
    start = 0
    for part in sums:
        cuts.append(joined[start : start + part.shape[0]])
        start += part.shape[0]
    qkv_b_g, outb_g, fc1_b_g, gain_g, beta_g = cuts
    return (
        block_out,
        input_grad,
        gain_g,
        beta_g,
        qkv_w_g,
        qkv_b_g.reshape(qkvb_sum.shape),
        out_w_g,
        outb_g,
        fc1_w_g,
        fc1_b_g,
        fc2_w_g,
        outb_g,
    )


def solution(mesh):
    rows = P(None, "context", "tensor")
    in_specs = (
        rows,
        P("tensor"),
        P("tensor"),
        P(None, "context", "tensor"),
        P(None, "tensor"),
        P("tensor", "context"),
        P("tensor"),
        P("context", "tensor"),
        P("tensor"),
        P("tensor", "context"),
        P("tensor"),
        P(),
        rows,
    )
    out_specs = (
        rows,
        rows,
        P("tensor"),
        P("tensor"),
        P(None, "context", "tensor"),
        P(None, "tensor"),
        P("tensor", "context"),
        P("tensor"),
        P("context", "tensor"),
        P("tensor"),
        P("tensor", "context"),
        P("tensor"),
    )
    return jax.shard_map(
        on_device, mesh=mesh, in_specs=in_specs, out_specs=out_specs, check_vma=False
    )
```

```python
import functools
import math

import jax
import jax.numpy as jnp
from jax import lax
from jax.experimental import pallas as pl
from jax.experimental.pallas import tpu as pltpu
from jax.sharding import PartitionSpec as P

HD = 64
ROT = 32

NORM_EPS = 1e-05
NEG_BIG = -1e30
GELU_COEF = 0.7978845608028654
GELU_CUBE = 0.044715

LANES = 128
VMEM = 60 * 1024 * 1024

f32 = jnp.float32
bf16 = jnp.bfloat16


def dot(spec, a, b):
    return jnp.einsum(spec, a, b, preferred_element_type=f32)


def gelu_and_slope(h):
    t = jnp.tanh(GELU_COEF * (h + GELU_CUBE * h * h * h))
    act = 0.5 * h * (1.0 + t)
    slope = 0.5 * (1.0 + t) + 0.5 * h * (1.0 - t * t) * GELU_COEF * (
        1.0 + 3.0 * GELU_CUBE * h * h
    )
    return act, slope


def swap(value, axis, mask):
    size = lax.axis_size(axis)
    return lax.ppermute(value, axis, [(i, i ^ mask) for i in range(size)])


def sum_over(value, axis):
    size = lax.axis_size(axis)
    if size & (size - 1):
        return lax.psum(value, axis)
    mask = 1
    while mask < size:
        value = value + swap(value, axis, mask)
        mask *= 2
    return value


def fence(*values):
    return lax.optimization_barrier(values)


class Rows:
    def __init__(self, seq_count, block_order):
        n_ctx = lax.axis_size("context")
        self.members = math.gcd(seq_count, n_ctx)
        self.groups = n_ctx // self.members
        self.per = seq_count // self.members
        self.all_order = block_order
        start = lax.axis_index("context") // self.members * self.members
        self.order = lax.dynamic_slice_in_dim(block_order, start, self.members)

    def _exchange(self, split):
        teams = None
        if self.groups > 1:
            teams = [
                [g * self.members + m for m in range(self.members)] for g in range(self.groups)
            ]
        return lax.all_to_all(split, "context", 0, 0, axis_index_groups=teams, tiled=True)

    def gather(self, rows):
        seqs, block, width = rows.shape
        got = self._exchange(rows.reshape(self.members, self.per, block, width))
        return got.swapaxes(0, 1).reshape(self.per * self.members * block, width)

    def scatter(self, rows):
        width = rows.shape[-1]
        split = rows.reshape(self.per, self.members, -1, width).swapaxes(0, 1)
        got = self._exchange(split)
        return got.reshape(self.members * self.per, split.shape[2], width)


def neighbours(small):
    return [small] + [swap(small, "tensor", m) for m in range(1, lax.axis_size("tensor"))]


def far_pieces(rows, near):
    half = rows.shape[0] // 2
    near_x, near_y = near
    far_top = swap(near_y[:half], "tensor", 1)
    far_low = swap(near_x[half:], "tensor", 2)
    return rows, near_x, near_y, far_top, far_low


def joined_kernel(place_ref, own, near_x, near_y, far_top, far_low, *rest):
    normed = len(rest) > 4
    width = own.shape[1]
    top = pl.program_id(0) < pl.num_programs(0) // 2
    far = jnp.where(top, far_top[...].astype(f32), far_low[...].astype(f32))
    pieces = [own[...].astype(f32), near_x[...].astype(f32), near_y[...].astype(f32), far]
    if normed:
        gain_ref, shift_ref, out_ref, out_c_ref, out_t_ref, out_o_ref = rest[:6]
        mean_ref, inv_ref = rest[6:]
        total = 4 * width
        mean = sum(jnp.sum(p, -1, keepdims=True) for p in pieces) / total
        centred = [p - mean for p in pieces]
        spread = sum(jnp.sum(c * c, -1, keepdims=True) for c in centred) / total
        inv = lax.rsqrt(spread + NORM_EPS)
        mean_ref[...] = mean
        inv_ref[...] = inv
        pieces = [
            c * inv * gain_ref[m : m + 1].astype(f32) + shift_ref[m : m + 1].astype(f32)
            for m, c in enumerate(centred)
        ]
    else:
        out_ref, out_c_ref, out_t_ref, out_o_ref = rest
    half = width // 2
    for m, piece in enumerate(pieces):
        owner = place_ref[0] ^ m
        out_ref[:, pl.ds(pl.multiple_of(owner * width, LANES), width)] = piece.astype(bf16)
        for c in range(2):
            slot = (place_ref[2] - owner) & 3
            at = pl.ds(pl.multiple_of(slot * half, LANES), half)
            side = place_ref[1] ^ c
            wide = pl.ds(pl.multiple_of((side * 4 + slot) * half, LANES), half)
            part = piece[:, c * half : (c + 1) * half]
            out_c_ref[:, wide] = part.astype(bf16)
            turned = part.T.astype(bf16)

            @pl.when(side == 0)
            def _(at=at, turned=turned):
                out_t_ref[at, :] = turned

            @pl.when(side == 1)
            def _(at=at, turned=turned):
                out_o_ref[at, :] = turned


def join_features(pieces, gains=None, shifts=None):
    rows, width = pieces[0].shape
    block = min(128, rows // 2)
    steps = rows // block
    ctx = lax.axis_index("context")
    place = jnp.stack([lax.axis_index("tensor"), ctx % 2, ctx // 2]).astype(jnp.int32)
    piece = pl.BlockSpec((block, width), lambda i, t: (i, 0))
    top = pl.BlockSpec((block, width), lambda i, t: (jnp.minimum(i, steps // 2 - 1), 0))
    low = pl.BlockSpec((block, width), lambda i, t: (jnp.maximum(i - steps // 2, 0), 0))
    in_specs = [piece] * 3 + [top, low]
    args = list(pieces)
    out_specs = [pl.BlockSpec((block, 4 * width), lambda i, t: (i, 0))] * 2
    out_specs += [pl.BlockSpec((2 * width, block), lambda i, t: (0, i))] * 2
    out_shape = [jax.ShapeDtypeStruct((rows, 4 * width), bf16)] * 2
    out_shape += [jax.ShapeDtypeStruct((2 * width, rows), bf16)] * 2
    if gains is not None:
        in_specs += [pl.BlockSpec((4, width), lambda i, t: (0, 0))] * 2
        args += [gains, shifts]
        out_specs += [pl.BlockSpec((block, 1), lambda i, t: (i, 0))] * 2
        out_shape += [jax.ShapeDtypeStruct((rows, 1), f32)] * 2
    out = pl.pallas_call(
        joined_kernel,
        grid_spec=pltpu.PrefetchScalarGridSpec(
            num_scalar_prefetch=1, grid=(steps,), in_specs=in_specs, out_specs=out_specs
        ),
        out_shape=out_shape,
        compiler_params=pltpu.CompilerParams(vmem_limit_bytes=VMEM),
        cost_estimate=pl.CostEstimate(
            flops=40 * rows * width, bytes_accessed=16 * rows * width, transcendentals=rows
        ),
    )(place, *args)
    return out


class FeatureSum:
    def __init__(self, chunks):
        self.chunks = chunks
        half = chunks.shape[1] // 2
        self.held = (
            swap(chunks[0, :half], "tensor", 1),
            swap(chunks[0, half:], "tensor", 2),
        )

    def step(self):
        via_x, via_y = self.held
        half = via_x.shape[0]

        def joined(value, via, top):
            ends = [value[:half].astype(f32), value[half:].astype(f32)]
            ends[0 if top else 1] += via.astype(f32)
            return jnp.concatenate(ends, 0).astype(bf16)

        from_y = swap(joined(self.chunks[1], via_x, True), "tensor", 2)
        from_x = swap(joined(self.chunks[2], via_y, False), "tensor", 1)
        self.held = from_x, from_y

    def total(self):
        from_x, from_y = self.held
        return self.chunks[3].astype(f32) + from_x.astype(f32) + from_y.astype(f32)


def hop(value, by, low, high):
    table = [(2 * i + c, 2 * (i + by) + c) for i in range(low, high + 1) for c in range(2)]
    return lax.ppermute(value, "context", table)


def merge_kernel(own_ref, *refs):
    out = refs[-1]
    part = own_ref.shape[1]
    out[:part, :] = own_ref[0]
    for slot in range(3):
        at = slice((slot + 1) * part, (slot + 2) * part)
        out[at, :] = refs[2 * slot][0] + refs[2 * slot + 1][0]


class Spread:
    def __init__(self, *own):
        self.own = jnp.stack(own)
        self.got = []

    def step(self):
        n = len(self.got)
        up, down = self.got[-1] if n else (self.own, self.own)
        self.got = self.got + [(hop(up, 1, n, 2), hop(down, -1, 1, 3 - n))]

    def joined(self, n):
        (up1, down1), (up2, down2), (up3, down3) = self.got
        _, part, cols = self.own.shape
        return pl.pallas_call(
            merge_kernel,
            grid=(cols // COLUMNS,),
            in_specs=[pl.BlockSpec((1, part, COLUMNS), lambda i: (n, 0, i))] * 7,
            out_specs=pl.BlockSpec((4 * part, COLUMNS), lambda i: (0, i)),
            out_shape=jax.ShapeDtypeStruct((4 * part, cols), bf16),
            compiler_params=pltpu.CompilerParams(vmem_limit_bytes=VMEM),
            cost_estimate=SHORT,
        )(self.own, up1, down3, up2, down2, up3, down1)


SHORT = pl.CostEstimate(flops=1, bytes_accessed=4 * 1024 * 1024, transcendentals=0)
COLUMNS = 512


def grad_kernel(tiles, *refs):
    given, outs = refs[: 4 * len(tiles)], refs[4 * len(tiles) :]
    part = outs[0].shape[0]
    first = 0
    for n, count in enumerate(tiles):
        own_ref, own_values, other_ref, other_values = given[4 * n : 4 * n + 4]
        step = pl.program_id(0)

        @pl.when((step >= first) & (step < first + count))
        def _(own=own_ref, own_v=own_values, other=other_ref, other_v=other_values):
            for slot in range(4):
                at = slice(slot * part, (slot + 1) * part)
                total = jnp.dot(own[at, :], own_v[...], preferred_element_type=f32)
                total += jnp.dot(other[at, :], other_v[...], preferred_element_type=f32)
                outs[slot][...] = total.astype(bf16)

        first += count


class ChainSum:
    def __init__(self, *products):
        half, count = products[0][2].shape
        tiles = [p[1].shape[1] // COLUMNS for p in products]
        in_specs, first = [], 0
        for number in tiles:
            rows = pl.BlockSpec((half, count), lambda i: (0, 0))
            values = pl.BlockSpec(
                (count, COLUMNS),
                lambda i, first=first, last=number - 1: (0, jnp.clip(i - first, 0, last)),
            )
            in_specs += [rows, values] * 2
            first += number
        moving = pl.BlockSpec((half // 4, COLUMNS), lambda i: (0, i))
        shape = jax.ShapeDtypeStruct((half // 4, first * COLUMNS), bf16)
        parts = pl.pallas_call(
            functools.partial(grad_kernel, tiles),
            grid=(first,),
            in_specs=in_specs,
            out_specs=[moving] * 4,
            out_shape=[shape] * 4,
            compiler_params=pltpu.CompilerParams(vmem_limit_bytes=VMEM),
            cost_estimate=SHORT,
        )(*(v for p in products for v in p))
        self.held = parts, ()

    def ready(self):
        parts, before = self.held
        n = len(before)
        up, down = parts[n + 1], parts[3 - n]
        if n:
            last_up, last_down = before[-1]
            up = (up.astype(f32) + last_up.astype(f32)).astype(bf16)
            down = (down.astype(f32) + last_down.astype(f32)).astype(bf16)
        return up, down

    def step(self, sends=None):
        parts, before = self.held
        n = len(before)
        up, down = sends or self.ready()
        self.held = parts, before + ((hop(up, 1, 0, n), hop(down, -1, 3 - n, 3)),)

    def total(self):
        parts, before = self.held
        up, down = before[-1]
        return parts[0].astype(f32) + up.astype(f32) + down.astype(f32)


def chunk_kernel(
    low, place_ref, wide_ref, long_ref, first_ref, mine_ref, other_ref, *rest
):
    summed = len(rest) > 1
    high = low + wide_ref.shape[1]
    half = mine_ref.shape[0]
    step = 256

    def mm(a, b):
        return lax.dot_general(a, b, (((1,), (1,)), ((), ())), preferred_element_type=f32)

    if summed:
        gain_ref, shift_ref, normed_ref, out_ref, sums_ref = rest

        @pl.when(pl.program_id(0) == 0)
        def _():
            sums_ref[...] = jnp.zeros_like(sums_ref)

    else:
        out_ref = rest[0]
    for c, weight_ref in enumerate((mine_ref, other_ref)):
        at = pl.ds(pl.multiple_of((place_ref[8] ^ c) * half, half), half)
        for start in range(0, wide_ref.shape[0], step):
            rows = slice(start, start + step)
            part = mm(wide_ref[rows, :], first_ref[at, low:high])
            part += mm(long_ref[rows, :], weight_ref[...])
            out_ref[0, rows, at] = part.astype(bf16)
            if summed:
                scaled = part * gain_ref[0, :, at].astype(f32)
                offset = normed_ref[rows, at].astype(f32) - shift_ref[0, :, at].astype(f32)
                sums_ref[0, rows, :] += jnp.sum(scaled, -1, keepdims=True)
                sums_ref[1, rows, :] += jnp.sum(part * offset, -1, keepdims=True)


def feature_chunks(place, wide, long, first, low, weight, norms=None):
    mine, other = weight
    rows = wide.shape[0]
    size = first.shape[0] // 4
    half = size // 2

    def resident(value):
        return pl.BlockSpec(value.shape, lambda i, p: (0, 0))

    def by_slot(value):
        return pl.BlockSpec((half, value.shape[1]), lambda i, p: (p[4 + i], 0))

    in_specs = [
        resident(wide),
        resident(long),
        pl.BlockSpec((size, first.shape[1]), lambda i, p: (p[i], 0)),
        by_slot(mine),
        by_slot(other),
    ]
    args = [wide, long, first, mine, other]
    out_specs = [pl.BlockSpec((1, rows, size), lambda i, p: (i, 0, 0))]
    out_shape = [jax.ShapeDtypeStruct((4, rows, size), bf16)]
    if norms is not None:
        gains, shifts, normed = norms
        line = pl.BlockSpec((1, 1, size), lambda i, p: (3 - i, 0, 0))
        in_specs += [line, line, pl.BlockSpec((rows, size), lambda i, p: (0, p[i]))]
        args += [gains[:, None, :], shifts[:, None, :], normed]
        out_specs += [pl.BlockSpec((2, rows, 1), lambda i, p: (0, 0, 0))]
        out_shape += [jax.ShapeDtypeStruct((2, rows, 1), f32)]
    out = pl.pallas_call(
        functools.partial(chunk_kernel, low),
        grid_spec=pltpu.PrefetchScalarGridSpec(
            num_scalar_prefetch=1, grid=(4,), in_specs=in_specs, out_specs=out_specs
        ),
        out_shape=out_shape,
        compiler_params=pltpu.CompilerParams(vmem_limit_bytes=VMEM),
        cost_estimate=SHORT,
    )(place, *args)
    return out if norms is not None else out[0]


def forward_kernel(rows_ref, mine_ref, other_ref, bias_ref, act_ref, slope_ref):
    half = mine_ref.shape[0]
    step = 256
    for start in range(0, rows_ref.shape[0], step):
        at = slice(start, start + step)
        h = jnp.dot(rows_ref[at, :half], mine_ref[...], preferred_element_type=f32)
        h += jnp.dot(rows_ref[at, half:], other_ref[...], preferred_element_type=f32)
        act, slope = gelu_and_slope(h + bias_ref[...].astype(f32))
        act_ref[at, :] = act.astype(bf16)
        slope_ref[at, :] = slope.astype(bf16)


def backward_kernel(rows_ref, mine_ref, other_ref, slope_ref, grad_ref, sum_ref):
    half = mine_ref.shape[0]
    step = 256
    total = jnp.zeros(sum_ref.shape, f32)
    for start in range(0, rows_ref.shape[0], step):
        at = slice(start, start + step)
        h = jnp.dot(rows_ref[at, :half], mine_ref[...], preferred_element_type=f32)
        h += jnp.dot(rows_ref[at, half:], other_ref[...], preferred_element_type=f32)
        h *= slope_ref[at, :].astype(f32)
        grad_ref[at, :] = h.astype(bf16)
        total += jnp.sum(h, axis=0, keepdims=True)
    sum_ref[...] = total


def hidden_layer(kernel, rows, weight, last, outs):
    mine, other = weight
    count, depth = rows.shape
    cols = mine.shape[1]
    tile = COLUMNS

    def spec(height):
        return pl.BlockSpec((height, tile), lambda i: (0, i))

    return pl.pallas_call(
        kernel,
        grid=(cols // tile,),
        in_specs=[
            pl.BlockSpec((count, depth), lambda i: (0, 0)),
            spec(depth // 2),
            spec(depth // 2),
            spec(last.shape[0]),
        ],
        out_specs=[spec(o.shape[0]) for o in outs],
        out_shape=outs,
        compiler_params=pltpu.CompilerParams(vmem_limit_bytes=VMEM),
        cost_estimate=SHORT,
    )(rows, mine, other, last)


def rotary_tables(length, lanes):
    half_rot = ROT // 2
    freqs = jnp.exp(jnp.arange(half_rot, dtype=f32) * (-2.0 * math.log(10000.0) / ROT))
    angles = jnp.arange(length, dtype=jnp.int32).astype(f32)[:, None] * freqs[None, :]
    cosine = jnp.cos(angles)
    sine = jnp.sin(angles)
    zero = jnp.zeros((length, half_rot), f32)
    rest_one = jnp.ones((length, HD - ROT), f32)
    rest_zero = jnp.zeros((length, HD - ROT), f32)
    keep = jnp.concatenate([cosine, cosine, rest_one], -1)
    from_high = jnp.concatenate([-sine, zero, rest_zero], -1)
    from_low = jnp.concatenate([zero, sine, rest_zero], -1)
    many = lanes // HD
    return jnp.stack([jnp.tile(v, (1, many)) for v in (keep, from_high, from_low)])


def attention_kernel(
    tile, slot_ref, q_ref, k_ref, v_ref, grad_ref, table_ref, attn_ref, dproj_ref, bias_ref, *scratch
):
    q_s, k_s, v_s, g_s, qt_s, kt_s, vt_s, gt_s, at_s, dqt_s, dk_s, dv_s = scratch
    length, lanes = q_ref.shape
    blocks = slot_ref.shape[0]
    block = length // blocks
    tiles = length // tile
    half_rot = ROT // 2
    scale = HD ** (-0.5)
    many = lanes // HD
    width = dproj_ref.shape[1] // 3

    def turn(u, at, sign):
        keep, high, low = table_ref[0, at, :], table_ref[1, at, :], table_ref[2, at, :]
        moved = pltpu.roll(u, lanes - half_rot, 1) * high + pltpu.roll(u, half_rot, 1) * low
        return u * keep + sign * moved

    def places(b):
        at = slice(b * block, (b + 1) * block)
        return at, pl.ds(pl.multiple_of(slot_ref[b] * block, block), block)

    for b in range(blocks):
        at, came = places(b)
        q = turn(q_ref[came, :], at, 1.0).astype(bf16).astype(f32) * scale
        k = turn(k_ref[came, :], at, 1.0).astype(bf16).astype(f32)
        v = v_ref[came, :].astype(bf16).astype(f32)
        g = grad_ref[came, :].astype(f32)
        for value, flat, turned in ((q, q_s, qt_s), (k, k_s, kt_s), (v, v_s, vt_s), (g, g_s, gt_s)):
            turned[:, at] = value.T.astype(bf16)
            for h in range(many):
                flat[h, at, :] = value[:, h * HD : (h + 1) * HD].astype(bf16)

    row = lax.broadcasted_iota(jnp.int32, (tile, tile), 0)
    col = lax.broadcasted_iota(jnp.int32, (tile, tile), 1)
    hidden = row > col

    def mm(a, b):
        return jnp.dot(a, b, preferred_element_type=f32)

    for h in range(many):
        feats = slice(h * HD, (h + 1) * HD)
        for i in range(tiles):
            qs = slice(i * tile, (i + 1) * tile)
            q_t = qt_s[feats, qs]
            scores = []
            for j in range(i + 1):
                s = mm(k_s[h, j * tile : (j + 1) * tile, :], q_t)
                scores.append(jnp.where(hidden, NEG_BIG, s) if j == i else s)
            top = functools.reduce(
                jnp.maximum, [jnp.max(s, axis=0, keepdims=True) for s in scores]
            )
            weights = [jnp.exp(s - top) for s in scores]
            total = functools.reduce(
                jnp.add, [jnp.sum(w, axis=0, keepdims=True) for w in weights]
            )
            mixed = functools.reduce(
                jnp.add,
                [
                    mm(vt_s[feats, j * tile : (j + 1) * tile], w.astype(bf16))
                    for j, w in enumerate(weights)
                ],
            )
            mixed = (mixed / total).astype(bf16).astype(f32)
            at_s[feats, qs] = mixed
            g_t = gt_s[feats, qs]
            delta = jnp.sum(g_t.astype(f32) * mixed, axis=0, keepdims=True)
            inverse = 1.0 / total
            dq = None
            for j in range(i + 1):
                ks = slice(j * tile, (j + 1) * tile)
                p = weights[j] * inverse
                dp = mm(v_s[h, ks, :], g_t)
                ds = (p * (dp - delta)).astype(bf16)
                dv = mm(p.astype(bf16), g_s[h, qs, :])
                dk = mm(ds, q_s[h, qs, :])
                if i == j:
                    dv_s[h, ks, :] = dv
                    dk_s[h, ks, :] = dk
                else:
                    dv_s[h, ks, :] += dv
                    dk_s[h, ks, :] += dk
                part = mm(kt_s[feats, ks], ds)
                dq = part if dq is None else dq + part
            dqt_s[feats, qs] = dq * scale

    sums = [jnp.zeros((1, lanes), f32) for _ in range(3)]
    for b in range(blocks):
        at, came = places(b)
        attn_ref[came, :] = at_s[:, at].T.astype(bf16)
        dq = turn(dqt_s[:, at].T, at, -1.0)
        dk = turn(jnp.concatenate([dk_s[h, at, :] for h in range(many)], 1), at, -1.0)
        dv = jnp.concatenate([dv_s[h, at, :] for h in range(many)], 1)
        for index, value in enumerate((dq, dk, dv)):
            lane = pl.multiple_of(index * width + pl.program_id(1) * lanes, lanes)
            dproj_ref[came, pl.ds(lane, lanes)] = value.astype(bf16)
            sums[index] = sums[index] + jnp.sum(value, axis=0, keepdims=True)
    for index in range(3):
        bias_ref[0, index] = sums[index]


def attention_whole(proj, attn_grad, plan, tables):
    rows = proj.shape[0]
    width = proj.shape[1] // 3
    per, members = plan.per, plan.members
    length = rows // per
    tile = min(256, length)
    many = LANES // HD
    steps = width // LANES
    slots = jnp.sum(
        jnp.where(
            plan.order[None, :] == jnp.arange(members, dtype=jnp.int32)[:, None],
            jnp.arange(members, dtype=jnp.int32)[None, :],
            0,
        ),
        axis=1,
    ).astype(jnp.int32)
    flat = pltpu.VMEM((many, length, HD), bf16)
    turned = pltpu.VMEM((LANES, length), bf16)
    wide = pltpu.VMEM((LANES, length), f32)
    sums = pltpu.VMEM((many, length, HD), f32)

    def columns(part):
        return pl.BlockSpec((length, LANES), lambda s, h, o: (s, part * steps + h))

    attn, dproj, bias = pl.pallas_call(
        functools.partial(attention_kernel, tile),
        grid_spec=pltpu.PrefetchScalarGridSpec(
            num_scalar_prefetch=1,
            grid=(per, steps),
            in_specs=[
                columns(0),
                columns(1),
                columns(2),
                columns(0),
                pl.BlockSpec((3, length, LANES), lambda s, h, o: (0, 0, 0)),
            ],
            out_specs=[
                columns(0),
                pl.BlockSpec((length, 3 * width), lambda s, h, o: (s, 0)),
                pl.BlockSpec((1, 3, 1, LANES), lambda s, h, o: (s, 0, 0, h)),
            ],
            scratch_shapes=[flat] * 4 + [turned] * 4 + [wide] * 2 + [sums] * 2,
        ),
        out_shape=[
            jax.ShapeDtypeStruct((rows, width), bf16),
            jax.ShapeDtypeStruct((rows, 3 * width), bf16),
            jax.ShapeDtypeStruct((per, 3, 1, width), f32),
        ],
        compiler_params=pltpu.CompilerParams(vmem_limit_bytes=VMEM),
        cost_estimate=SHORT,
    )(slots, proj, proj, proj, attn_grad, tables)
    return attn, dproj, jnp.sum(bias, axis=(0, 2)).reshape(-1)


def rotate(values, cosine, sine):
    half_rot = ROT // 2
    front = values[..., :ROT]
    turned = jnp.concatenate([-front[..., half_rot:], front[..., :half_rot]], -1)
    return jnp.concatenate([front * cosine + turned * sine, values[..., ROT:]], -1)


def rotate_back(grads, cosine, sine):
    half_rot = ROT // 2
    front = grads[..., :ROT]
    by_sine = front * sine
    turned = jnp.concatenate([by_sine[..., half_rot:], -by_sine[..., :half_rot]], -1)
    return jnp.concatenate([front * cosine + turned, grads[..., ROT:]], -1)


def attention_split(proj, attn_grad, plan, block_len):
    rows = attn_grad.shape[0]
    width = attn_grad.shape[1]
    per, members, groups = plan.per, plan.members, plan.groups
    count = rows // per
    heads = width // HD

    def positions(blocks):
        inside = jnp.arange(block_len, dtype=jnp.int32)
        return (blocks[:, None] * block_len + inside[None, :]).reshape(-1)

    position = positions(plan.order)
    every = positions(plan.all_order)
    half_rot = ROT // 2
    freqs = jnp.exp(jnp.arange(half_rot, dtype=f32) * (-2.0 * math.log(10000.0) / ROT))
    angles = position.astype(f32)[:, None] * freqs[None, :]
    cosine = jnp.concatenate([jnp.cos(angles)] * 2, -1)[None, :, None, :]
    sine = jnp.concatenate([jnp.sin(angles)] * 2, -1)[None, :, None, :]
    teams = [[m + members * g for g in range(groups)] for m in range(members)]

    def team_gather(value, axis):
        return lax.all_gather(
            value, "context", axis=axis, tiled=True, axis_index_groups=teams
        )

    def team_sum(value):
        return lax.psum_scatter(
            value, "context", scatter_dimension=1, tiled=True, axis_index_groups=teams
        )

    shape = (per, count, heads, HD)
    q = rotate(proj[:, :width].reshape(shape), cosine, sine).astype(bf16)
    k = rotate(proj[:, width : 2 * width].reshape(shape), cosine, sine).astype(bf16)
    v = proj[:, 2 * width :].reshape(shape).astype(bf16)
    g = attn_grad.reshape(shape)
    k_all = team_gather(k, 1)
    v_all = team_gather(v, 1)
    visible = every[None, :] <= position[:, None]
    scale = HD ** (-0.5)
    outs, dqs, dks, dvs = [], [], [], []
    for h in range(heads):
        s = dot("sqd,skd->sqk", q[:, :, h], k_all[:, :, h]) * scale
        s = jnp.where(visible, s, NEG_BIG)
        top = jnp.max(s, -1, keepdims=True)
        e = jnp.where(visible, jnp.exp(s - top), 0.0)
        total = jnp.sum(e, -1, keepdims=True)
        o = (dot("sqk,skd->sqd", e.astype(bf16), v_all[:, :, h]) / total).astype(bf16)
        delta = jnp.sum(g[:, :, h].astype(f32) * o.astype(f32), -1, keepdims=True)
        p = e / total
        dp = dot("sqd,skd->sqk", g[:, :, h], v_all[:, :, h])
        ds = (p * (dp - delta) * scale).astype(bf16)
        outs.append(o)
        dqs.append(dot("sqk,skd->sqd", ds, k_all[:, :, h]))
        dks.append(dot("sqk,sqd->skd", ds, q[:, :, h]))
        dvs.append(dot("sqk,sqd->skd", p.astype(bf16), g[:, :, h]))
    attn = jnp.concatenate(outs, -1).reshape(rows, width)
    dq = rotate_back(jnp.stack(dqs, 2), cosine, sine).reshape(rows, width)
    dk = team_sum(jnp.concatenate(dks, -1)).reshape(shape)
    dk = rotate_back(dk, cosine, sine).reshape(rows, width)
    dv = team_sum(jnp.concatenate(dvs, -1)).reshape(rows, width)
    dproj = jnp.concatenate([dq, dk, dv], -1)
    return attn, dproj.astype(bf16), jnp.sum(dproj, axis=0)


def general_block(
    block_in,
    norm_gain,
    layer_norm_bias,
    qkv_weight,
    qkv_bias,
    out_weight,
    out_bias,
    fc1_weight,
    fc1_bias,
    fc2_weight,
    fc2_bias,
    block_order,
    out_grad,
):
    seq_count, block_len, width = block_in.shape
    plan = Rows(seq_count, block_order)
    x_own = plan.gather(block_in)
    g_own = plan.gather(out_grad)
    qkv_flat = qkv_weight.swapaxes(0, 1).reshape(qkv_weight.shape[1], -1)
    qkv_full = lax.all_gather(qkv_flat, "context", axis=0, tiled=True)
    out_full = lax.all_gather(out_weight, "context", axis=1, tiled=True)
    fc1_full = lax.all_gather(fc1_weight, "context", axis=0, tiled=True)
    fc2_full = lax.all_gather(fc2_weight, "context", axis=1, tiled=True)
    x_full, g_full, gain, shift = (
        lax.all_gather(v, "tensor", axis=v.ndim - 1, tiled=True)
        for v in (x_own, g_own, norm_gain, layer_norm_bias)
    )
    centred = x_full.astype(f32)
    mean = jnp.mean(centred, -1, keepdims=True)
    centred = centred - mean
    inv_std = lax.rsqrt(jnp.mean(centred * centred, -1, keepdims=True) + NORM_EPS)
    xhat = centred * inv_std
    normed = (xhat * gain.astype(f32) + shift.astype(f32)).astype(bf16)

    proj = dot("rd,de->re", normed, qkv_full) + qkv_bias.astype(f32).reshape(-1)
    attn_grad = dot("rd,ed->re", g_full, out_full).astype(bf16)
    if plan.groups == 1:
        tables = rotary_tables(proj.shape[0] // plan.per, LANES)
        attn, dproj, qkvb_sum = attention_whole(proj, attn_grad, plan, tables)
    else:
        attn, dproj, qkvb_sum = attention_split(proj, attn_grad, plan, block_len)
    hidden_pre = dot("rd,df->rf", normed, fc1_full) + fc1_bias.astype(f32)
    hidden_act, slope = gelu_and_slope(hidden_pre)
    hidden_act = hidden_act.astype(bf16)
    hidden_grad = dot("rd,fd->rf", g_full, fc2_full) * slope
    fc1b_sum = jnp.sum(hidden_grad, axis=0)
    hidden_grad = hidden_grad.astype(bf16)

    def rows_summed(part):
        part = part.astype(bf16)
        return lax.psum_scatter(part, "context", scatter_dimension=0, tiled=True).astype(f32)

    qkv_w_g = rows_summed(dot("rd,re->de", normed, dproj))
    out_w_g = rows_summed(dot("rd,re->de", g_full, attn))
    fc2_w_g = rows_summed(dot("rd,rf->df", g_full, hidden_act))
    fc1_w_g = rows_summed(dot("rd,rf->df", normed, hidden_grad))

    def features_summed(value):
        value = value.astype(bf16)
        return lax.psum_scatter(value, "tensor", scatter_dimension=1, tiled=True).astype(f32)

    part = dot("re,de->rd", dproj, qkv_full) + dot("rf,df->rd", hidden_grad, fc1_full)
    scaled = part * gain.astype(f32)
    row_sums = jnp.stack([jnp.sum(scaled, -1), jnp.sum(scaled * xhat, -1)])
    row_sums = sum_over(row_sums, "tensor")
    norm_own = features_summed(part)
    branch = features_summed(
        dot("re,ed->rd", attn, out_full) + dot("rf,fd->rd", hidden_act, fc2_full)
    )
    change, sums = row_change(x_own, mean, inv_std, row_sums, norm_own, norm_gain)
    return finish(
        (block_in, out_grad, out_bias, fc2_bias, qkv_bias),
        (plan.scatter(change), plan.scatter(branch.astype(bf16))),
        (qkvb_sum, fc1b_sum, *sums),
        (jnp.concatenate([qkv_w_g, out_w_g], 1), 3 * width, fc1_w_g, fc2_w_g),
    )


def row_change(x_own, mean, inv_std, row_sums, norm_own, norm_gain):
    xhat_own = (x_own.astype(f32) - mean) * inv_std
    row_means = row_sums / (x_own.shape[1] * lax.axis_size("tensor"))
    change = inv_std * (
        norm_own * norm_gain.astype(f32)
        - row_means[0][:, None]
        - xhat_own * row_means[1][:, None]
    )
    sums = jnp.sum(norm_own * xhat_own, axis=0), jnp.sum(norm_own, axis=0)
    return change.astype(bf16), sums


def finish(given, rows, bias_sums, weights):
    block_in, out_grad, out_bias, fc2_bias, qkv_bias = given
    change, branch = rows
    qkvb_sum, fc1b_sum, gain_sum, beta_sum = bias_sums
    attn_w_g, qkv_width, fc1_w_g, fc2_w_g = weights
    width = block_in.shape[-1]
    block_out = (
        block_in.astype(f32)
        + branch.astype(f32)
        + out_bias.astype(f32)
        + fc2_bias.astype(f32)
    ).astype(bf16)
    grad_own = out_grad.astype(f32)
    input_grad = grad_own + change.astype(f32)

    outb_sum = jnp.sum(grad_own, axis=(0, 1))
    sums = (qkvb_sum, outb_sum, fc1b_sum, gain_sum, beta_sum)
    joined = sum_over(jnp.concatenate(sums), "context")
    cuts = []
    start = 0
    for part in sums:
        cuts.append(joined[start : start + part.shape[0]])
        start += part.shape[0]
    qkv_b_g, outb_g, fc1_b_g, gain_g, beta_g = cuts
    return (
        block_out,
        input_grad,
        gain_g,
        beta_g,
        attn_w_g[:, :qkv_width].reshape(-1, 3, width).swapaxes(0, 1),
        qkv_b_g.reshape(qkv_bias.shape),
        attn_w_g[:, qkv_width:].T,
        outb_g,
        fc1_w_g,
        fc1_b_g,
        fc2_w_g.T,
        outb_g,
    )


def staged_block(
    block_in,
    norm_gain,
    layer_norm_bias,
    qkv_weight,
    qkv_bias,
    out_weight,
    out_bias,
    fc1_weight,
    fc1_bias,
    fc2_weight,
    fc2_bias,
    block_order,
    out_grad,
):
    seq_count, block_len, width = block_in.shape
    plan = Rows(seq_count, block_order)
    ctx = lax.axis_index("context")
    z, k = ctx // 2, ctx % 2
    ten = lax.axis_index("tensor")
    qkv_width = 3 * width

    norm_pieces = neighbours(jnp.stack([norm_gain, layer_norm_bias]))
    x_own = plan.gather(block_in)
    first = jnp.concatenate(
        [qkv_weight.swapaxes(0, 1).reshape(qkv_weight.shape[1], -1), out_weight.T], 1
    )
    fc2_own = fc2_weight.T
    tables = rotary_tables(plan.members * block_len, LANES)
    x_own, norm_pieces, first, fc2_own, grad_in, tables = fence(
        x_own, norm_pieces, first, fc2_own, out_grad, tables
    )
    first_full = lax.all_gather(first, "context", axis=0, tiled=True)
    g_own = plan.gather(grad_in)
    near = [swap(x_own, "tensor", m) for m in (1, 2)]
    spread = Spread(fc1_weight, fc2_own)
    x_pieces, g_own, spread.own = fence(far_pieces(x_own, near), g_own, spread.own)
    spread.step()
    near = [swap(g_own, "tensor", m) for m in (1, 2)]
    gains = jnp.stack([p[0] for p in norm_pieces])
    shifts = jnp.stack([p[1] for p in norm_pieces])
    g_pieces = far_pieces(g_own, near)
    normed, normed_c, normed_t, normed_o, mean, inv_std = join_features(
        x_pieces, gains, shifts
    )
    g_full, g_c, g_t, g_o = join_features(g_pieces)
    first_full, normed, normed_c, normed_t, normed_o, g_full, g_c, g_t, g_o = fence(
        first_full, normed, normed_c, normed_t, normed_o, g_full, g_c, g_t, g_o
    )
    first_full, spread.got = fence(first_full, spread.got)
    qkv_full = first_full[:, :qkv_width]
    out_full = first_full[:, qkv_width:]

    spread.step()
    normed_o, g_o = swap(normed_o, "context", 1), swap(g_o, "context", 1)
    proj = dot("rd,de->re", normed, qkv_full) + qkv_bias.astype(f32).reshape(-1)
    attn_grad = dot("rd,de->re", g_full, out_full).astype(bf16)
    attn, dproj, qkvb_sum = attention_whole(proj, attn_grad, plan, tables)
    spread.got, attn, dproj, normed_o, g_o = fence(spread.got, attn, dproj, normed_o, g_o)

    spread.step()
    attn_sum = ChainSum(
        (normed_t, dproj, normed_o, swap(dproj, "context", 1)),
        (g_t, attn, g_o, swap(attn, "context", 1)),
    )
    (attn_sum.held,) = fence(attn_sum.held)

    attn_sum.step()
    spread.got, attn_sum.held = fence(spread.got, attn_sum.held)

    fc1_mine, sends = fence(spread.joined(0), attn_sum.ready())
    attn_sum.step(sends)
    fc1_full = fc1_mine, swap(fc1_mine, "context", 1)
    fc1_full, attn_sum.held = fence(fc1_full, attn_sum.held)

    attn_sum.step()
    wide = jax.ShapeDtypeStruct((normed_c.shape[0], fc1_bias.shape[0]), bf16)
    hidden_act, slope = hidden_layer(
        forward_kernel, normed_c, fc1_full, fc1_bias.reshape(1, -1), [wide, wide]
    )
    spread.got, hidden_act, slope, attn_sum.held = fence(
        spread.got, hidden_act, slope, attn_sum.held
    )

    hidden_o = swap(hidden_act, "context", 1)
    fc2_mine, hidden_o = fence(spread.joined(1), hidden_o)
    fc2_full = fc2_mine, swap(fc2_mine, "context", 1)
    fc2_sum = ChainSum((g_t, hidden_act, g_o, hidden_o))
    fc2_full, fc2_sum.held = fence(fc2_full, fc2_sum.held)

    fc2_sum.step()
    line = jax.ShapeDtypeStruct((1, fc1_bias.shape[0]), f32)
    hidden_grad, fc1b_sum = hidden_layer(
        backward_kernel, g_c, fc2_full, slope, [wide, line]
    )
    fc1b_sum = fc1b_sum.reshape(-1)
    fc2_sum.held, hidden_grad, attn = fence(fc2_sum.held, hidden_grad, attn)

    masks = jnp.arange(3, -1, -1, dtype=jnp.int32)
    owners = ten.astype(jnp.int32) ^ masks
    place = jnp.concatenate([owners, (z - owners) & 3, k.reshape(1)]).astype(jnp.int32)
    fc2_sum.step()
    hidden_grad_o = swap(hidden_grad, "context", 1)
    chunks = feature_chunks(place, attn, hidden_act, first_full, qkv_width, fc2_full)
    fc2_sum.held, hidden_grad_o, chunks = fence(fc2_sum.held, hidden_grad_o, chunks)

    fc2_sum.step()
    branch_sum = FeatureSum(chunks)
    fc1_sum = ChainSum((normed_t, hidden_grad, normed_o, hidden_grad_o))
    fc2_sum.held, branch_sum.held, fc1_sum.held, dproj = fence(
        fc2_sum.held, branch_sum.held, fc1_sum.held, dproj
    )

    fc1_sum.step()
    branch_sum.step()
    norm_chunks, row_sums = feature_chunks(
        place, dproj, hidden_grad, first_full, 0, fc1_full, (gains, shifts, normed)
    )
    fc1_sum.held, branch_sum.held, norm_chunks, row_sums = fence(
        fc1_sum.held, branch_sum.held, norm_chunks, row_sums
    )

    sends = fc1_sum.ready()
    branch = branch_sum.total().astype(bf16)
    sends, branch, norm_chunks, row_sums = fence(sends, branch, norm_chunks, row_sums)
    fc1_sum.step(sends)
    norm_sum = FeatureSum(norm_chunks)
    branch = plan.scatter(branch)
    row_sums = sum(neighbours(row_sums[..., 0]))
    attn_w_g = attn_sum.total()
    norm_sum.held, row_sums, attn_w_g = fence(norm_sum.held, row_sums, attn_w_g)
    norm_sum.step()
    fc2_w_g = fc2_sum.total()
    fc1_sum.held, norm_sum.held, fc2_w_g = fence(fc1_sum.held, norm_sum.held, fc2_w_g)

    sends = fc1_sum.ready()
    change, sums = row_change(x_own, mean, inv_std, row_sums, norm_sum.total(), norm_gain)
    sends, change, branch = fence(sends, change, branch)
    fc1_sum.step(sends)
    change = plan.scatter(change)
    return finish(
        (block_in, out_grad, out_bias, fc2_bias, qkv_bias),
        (change, branch),
        (qkvb_sum, fc1b_sum, *sums),
        (attn_w_g, qkv_width, fc1_sum.total(), fc2_w_g),
    )


def on_device(*args):
    block_in, block_order = args[0], args[11]
    four = lax.axis_size("context") == 8 and lax.axis_size("tensor") == 4
    if four and block_in.shape[0] % 8 == 0:
        return staged_block(*args)
    return general_block(*args)


def solution(mesh):
    rows = P(None, "context", "tensor")
    in_specs = (
        rows,
        P("tensor"),
        P("tensor"),
        P(None, "context", "tensor"),
        P(None, "tensor"),
        P("tensor", "context"),
        P("tensor"),
        P("context", "tensor"),
        P("tensor"),
        P("tensor", "context"),
        P("tensor"),
        P(),
        rows,
    )
    out_specs = (
        rows,
        rows,
        P("tensor"),
        P("tensor"),
        P(None, "context", "tensor"),
        P(None, "tensor"),
        P("tensor", "context"),
        P("tensor"),
        P("context", "tensor"),
        P("tensor"),
        P("tensor", "context"),
        P("tensor"),
    )
    return jax.shard_map(
        on_device, mesh=mesh, in_specs=in_specs, out_specs=out_specs, check_vma=False
    )
```

```python
import functools
import math

import jax
import jax.numpy as jnp
from jax import lax
from jax.experimental import pallas as pl
from jax.experimental.pallas import tpu as pltpu
from jax.sharding import PartitionSpec as P

HD = 64
ROT = 32

NORM_EPS = 1e-05
NEG_BIG = -1e30
GELU_COEF = 0.7978845608028654
GELU_CUBE = 0.044715

LANES = 128
VMEM = 60 * 1024 * 1024

f32 = jnp.float32
bf16 = jnp.bfloat16


def dot(spec, a, b):
    return jnp.einsum(spec, a, b, preferred_element_type=f32)


def gelu_and_slope(h):
    t = jnp.tanh(GELU_COEF * (h + GELU_CUBE * h * h * h))
    act = 0.5 * h * (1.0 + t)
    slope = 0.5 * (1.0 + t) + 0.5 * h * (1.0 - t * t) * GELU_COEF * (
        1.0 + 3.0 * GELU_CUBE * h * h
    )
    return act, slope


def swap(value, axis, mask):
    size = lax.axis_size(axis)
    return lax.ppermute(value, axis, [(i, i ^ mask) for i in range(size)])


def sum_over(value, axis):
    size = lax.axis_size(axis)
    if size & (size - 1):
        return lax.psum(value, axis)
    mask = 1
    while mask < size:
        value = value + swap(value, axis, mask)
        mask *= 2
    return value


def fence(*values):
    return lax.optimization_barrier(values)


class Rows:
    def __init__(self, seq_count, block_order):
        n_ctx = lax.axis_size("context")
        self.members = math.gcd(seq_count, n_ctx)
        self.groups = n_ctx // self.members
        self.per = seq_count // self.members
        self.all_order = block_order
        start = lax.axis_index("context") // self.members * self.members
        self.order = lax.dynamic_slice_in_dim(block_order, start, self.members)

    def _exchange(self, split):
        teams = None
        if self.groups > 1:
            teams = [
                [g * self.members + m for m in range(self.members)] for g in range(self.groups)
            ]
        return lax.all_to_all(split, "context", 0, 0, axis_index_groups=teams, tiled=True)

    def gather(self, rows):
        seqs, block, width = rows.shape
        got = self._exchange(rows.reshape(self.members, self.per, block, width))
        return got.swapaxes(0, 1).reshape(self.per * self.members * block, width)

    def scatter(self, rows):
        width = rows.shape[-1]
        split = rows.reshape(self.per, self.members, -1, width).swapaxes(0, 1)
        got = self._exchange(split)
        return got.reshape(self.members * self.per, split.shape[2], width)


def neighbours(small):
    return [small] + [swap(small, "tensor", m) for m in range(1, lax.axis_size("tensor"))]


def far_pieces(rows, near):
    half = rows.shape[0] // 2
    near_x, near_y = near
    far_top = swap(near_y[:half], "tensor", 1)
    far_low = swap(near_x[half:], "tensor", 2)
    return rows, near_x, near_y, far_top, far_low


def joined_kernel(place_ref, own, near_x, near_y, far_top, far_low, *rest):
    normed = len(rest) > 4
    width = own.shape[1]
    top = pl.program_id(0) < pl.num_programs(0) // 2
    far = jnp.where(top, far_top[...].astype(f32), far_low[...].astype(f32))
    pieces = [own[...].astype(f32), near_x[...].astype(f32), near_y[...].astype(f32), far]
    if normed:
        gain_ref, shift_ref, out_ref, out_c_ref, out_t_ref, out_o_ref = rest[:6]
        mean_ref, inv_ref = rest[6:]
        total = 4 * width
        mean = sum(jnp.sum(p, -1, keepdims=True) for p in pieces) / total
        centred = [p - mean for p in pieces]
        spread = sum(jnp.sum(c * c, -1, keepdims=True) for c in centred) / total
        inv = lax.rsqrt(spread + NORM_EPS)
        mean_ref[...] = mean
        inv_ref[...] = inv
        pieces = [
            c * inv * gain_ref[m : m + 1].astype(f32) + shift_ref[m : m + 1].astype(f32)
            for m, c in enumerate(centred)
        ]
    else:
        out_ref, out_c_ref, out_t_ref, out_o_ref = rest
    half = width // 2
    for m, piece in enumerate(pieces):
        owner = place_ref[0] ^ m
        out_ref[:, pl.ds(pl.multiple_of(owner * width, LANES), width)] = piece.astype(bf16)
        for c in range(2):
            slot = (place_ref[2] - owner) & 3
            at = pl.ds(pl.multiple_of(slot * half, LANES), half)
            side = place_ref[1] ^ c
            wide = pl.ds(pl.multiple_of((side * 4 + slot) * half, LANES), half)
            part = piece[:, c * half : (c + 1) * half]
            out_c_ref[:, wide] = part.astype(bf16)
            turned = part.T.astype(bf16)

            @pl.when(side == 0)
            def _(at=at, turned=turned):
                out_t_ref[at, :] = turned

            @pl.when(side == 1)
            def _(at=at, turned=turned):
                out_o_ref[at, :] = turned


def join_features(pieces, gains=None, shifts=None):
    rows, width = pieces[0].shape
    block = min(128, rows // 2)
    steps = rows // block
    ctx = lax.axis_index("context")
    place = jnp.stack([lax.axis_index("tensor"), ctx % 2, ctx // 2]).astype(jnp.int32)
    piece = pl.BlockSpec((block, width), lambda i, t: (i, 0))
    top = pl.BlockSpec((block, width), lambda i, t: (jnp.minimum(i, steps // 2 - 1), 0))
    low = pl.BlockSpec((block, width), lambda i, t: (jnp.maximum(i - steps // 2, 0), 0))
    in_specs = [piece] * 3 + [top, low]
    args = list(pieces)
    out_specs = [pl.BlockSpec((block, 4 * width), lambda i, t: (i, 0))] * 2
    out_specs += [pl.BlockSpec((2 * width, block), lambda i, t: (0, i))] * 2
    out_shape = [jax.ShapeDtypeStruct((rows, 4 * width), bf16)] * 2
    out_shape += [jax.ShapeDtypeStruct((2 * width, rows), bf16)] * 2
    if gains is not None:
        in_specs += [pl.BlockSpec((4, width), lambda i, t: (0, 0))] * 2
        args += [gains, shifts]
        out_specs += [pl.BlockSpec((block, 1), lambda i, t: (i, 0))] * 2
        out_shape += [jax.ShapeDtypeStruct((rows, 1), f32)] * 2
    out = pl.pallas_call(
        joined_kernel,
        grid_spec=pltpu.PrefetchScalarGridSpec(
            num_scalar_prefetch=1, grid=(steps,), in_specs=in_specs, out_specs=out_specs
        ),
        out_shape=out_shape,
        compiler_params=pltpu.CompilerParams(vmem_limit_bytes=VMEM),
        cost_estimate=pl.CostEstimate(
            flops=40 * rows * width, bytes_accessed=16 * rows * width, transcendentals=rows
        ),
    )(place, *args)
    return out


class FeatureSum:
    def __init__(self, chunks):
        self.chunks = chunks
        half = chunks.shape[1] // 2
        self.held = (
            swap(chunks[0, :half], "tensor", 1),
            swap(chunks[0, half:], "tensor", 2),
        )

    def step(self):
        via_x, via_y = self.held
        half = via_x.shape[0]

        def joined(value, via, top):
            ends = [value[:half].astype(f32), value[half:].astype(f32)]
            ends[0 if top else 1] += via.astype(f32)
            return jnp.concatenate(ends, 0).astype(bf16)

        from_y = swap(joined(self.chunks[1], via_x, True), "tensor", 2)
        from_x = swap(joined(self.chunks[2], via_y, False), "tensor", 1)
        self.held = from_x, from_y

    def total(self):
        from_x, from_y = self.held
        return self.chunks[3].astype(f32) + from_x.astype(f32) + from_y.astype(f32)


def hop(value, by, low, high):
    table = [(2 * i + c, 2 * (i + by) + c) for i in range(low, high + 1) for c in range(2)]
    return lax.ppermute(value, "context", table)


def merge_kernel(own_ref, *refs):
    out = refs[-1]
    part = own_ref.shape[1]
    out[:part, :] = own_ref[0]
    for slot in range(3):
        at = slice((slot + 1) * part, (slot + 2) * part)
        out[at, :] = refs[2 * slot][0] + refs[2 * slot + 1][0]


class Spread:
    def __init__(self, *own):
        self.own = jnp.stack(own)
        self.got = []

    def step(self):
        n = len(self.got)
        up, down = self.got[-1] if n else (self.own, self.own)
        self.got = self.got + [(hop(up, 1, n, 2), hop(down, -1, 1, 3 - n))]

    def joined(self, n):
        (up1, down1), (up2, down2), (up3, down3) = self.got
        _, part, cols = self.own.shape
        return pl.pallas_call(
            merge_kernel,
            grid=(cols // COLUMNS,),
            in_specs=[pl.BlockSpec((1, part, COLUMNS), lambda i: (n, 0, i))] * 7,
            out_specs=pl.BlockSpec((4 * part, COLUMNS), lambda i: (0, i)),
            out_shape=jax.ShapeDtypeStruct((4 * part, cols), bf16),
            compiler_params=pltpu.CompilerParams(vmem_limit_bytes=VMEM),
            cost_estimate=SHORT,
        )(self.own, up1, down3, up2, down2, up3, down1)


SHORT = pl.CostEstimate(flops=1, bytes_accessed=4 * 1024 * 1024, transcendentals=0)
COLUMNS = 512


def grad_kernel(tiles, *refs):
    given, outs = refs[: 4 * len(tiles)], refs[4 * len(tiles) :]
    part = outs[0].shape[0]
    first = 0
    for n, count in enumerate(tiles):
        own_ref, own_values, other_ref, other_values = given[4 * n : 4 * n + 4]
        step = pl.program_id(0)

        @pl.when((step >= first) & (step < first + count))
        def _(own=own_ref, own_v=own_values, other=other_ref, other_v=other_values):
            for slot in range(4):
                at = slice(slot * part, (slot + 1) * part)
                total = jnp.dot(own[at, :], own_v[...], preferred_element_type=f32)
                total += jnp.dot(other[at, :], other_v[...], preferred_element_type=f32)
                outs[slot][...] = total.astype(bf16)

        first += count


class ChainSum:
    def __init__(self, *products):
        half, count = products[0][2].shape
        tiles = [p[1].shape[1] // COLUMNS for p in products]
        in_specs, first = [], 0
        for number in tiles:
            rows = pl.BlockSpec((half, count), lambda i: (0, 0))
            values = pl.BlockSpec(
                (count, COLUMNS),
                lambda i, first=first, last=number - 1: (0, jnp.clip(i - first, 0, last)),
            )
            in_specs += [rows, values] * 2
            first += number
        moving = pl.BlockSpec((half // 4, COLUMNS), lambda i: (0, i))
        shape = jax.ShapeDtypeStruct((half // 4, first * COLUMNS), bf16)
        parts = pl.pallas_call(
            functools.partial(grad_kernel, tiles),
            grid=(first,),
            in_specs=in_specs,
            out_specs=[moving] * 4,
            out_shape=[shape] * 4,
            compiler_params=pltpu.CompilerParams(vmem_limit_bytes=VMEM),
            cost_estimate=SHORT,
        )(*(v for p in products for v in p))
        self.held = parts, ()

    def ready(self):
        parts, before = self.held
        n = len(before)
        up, down = parts[n + 1], parts[3 - n]
        if n:
            last_up, last_down = before[-1]
            up = (up.astype(f32) + last_up.astype(f32)).astype(bf16)
            down = (down.astype(f32) + last_down.astype(f32)).astype(bf16)
        return up, down

    def step(self, sends=None):
        parts, before = self.held
        n = len(before)
        up, down = sends or self.ready()
        self.held = parts, before + ((hop(up, 1, 0, n), hop(down, -1, 3 - n, 3)),)

    def total(self):
        parts, before = self.held
        up, down = before[-1]
        return parts[0].astype(f32) + up.astype(f32) + down.astype(f32)


def chunk_kernel(
    low, place_ref, wide_ref, long_ref, first_ref, mine_ref, other_ref, *rest
):
    summed = len(rest) > 1
    high = low + wide_ref.shape[1]
    half = mine_ref.shape[0]
    step = 256

    def mm(a, b):
        return lax.dot_general(a, b, (((1,), (1,)), ((), ())), preferred_element_type=f32)

    if summed:
        gain_ref, shift_ref, normed_ref, out_ref, sums_ref = rest

        @pl.when(pl.program_id(0) == 0)
        def _():
            sums_ref[...] = jnp.zeros_like(sums_ref)

    else:
        out_ref = rest[0]
    for c, weight_ref in enumerate((mine_ref, other_ref)):
        at = pl.ds(pl.multiple_of((place_ref[8] ^ c) * half, half), half)
        for start in range(0, wide_ref.shape[0], step):
            rows = slice(start, start + step)
            part = mm(wide_ref[rows, :], first_ref[at, low:high])
            part += mm(long_ref[rows, :], weight_ref[...])
            out_ref[0, rows, at] = part.astype(bf16)
            if summed:
                scaled = part * gain_ref[0, :, at].astype(f32)
                offset = normed_ref[rows, at].astype(f32) - shift_ref[0, :, at].astype(f32)
                sums_ref[0, rows, :] += jnp.sum(scaled, -1, keepdims=True)
                sums_ref[1, rows, :] += jnp.sum(part * offset, -1, keepdims=True)


def feature_chunks(place, wide, long, first, low, weight, norms=None):
    mine, other = weight
    rows = wide.shape[0]
    size = first.shape[0] // 4
    half = size // 2

    def resident(value):
        return pl.BlockSpec(value.shape, lambda i, p: (0, 0))

    def by_slot(value):
        return pl.BlockSpec((half, value.shape[1]), lambda i, p: (p[4 + i], 0))

    in_specs = [
        resident(wide),
        resident(long),
        pl.BlockSpec((size, first.shape[1]), lambda i, p: (p[i], 0)),
        by_slot(mine),
        by_slot(other),
    ]
    args = [wide, long, first, mine, other]
    out_specs = [pl.BlockSpec((1, rows, size), lambda i, p: (i, 0, 0))]
    out_shape = [jax.ShapeDtypeStruct((4, rows, size), bf16)]
    if norms is not None:
        gains, shifts, normed = norms
        line = pl.BlockSpec((1, 1, size), lambda i, p: (3 - i, 0, 0))
        in_specs += [line, line, pl.BlockSpec((rows, size), lambda i, p: (0, p[i]))]
        args += [gains[:, None, :], shifts[:, None, :], normed]
        out_specs += [pl.BlockSpec((2, rows, 1), lambda i, p: (0, 0, 0))]
        out_shape += [jax.ShapeDtypeStruct((2, rows, 1), f32)]
    out = pl.pallas_call(
        functools.partial(chunk_kernel, low),
        grid_spec=pltpu.PrefetchScalarGridSpec(
            num_scalar_prefetch=1, grid=(4,), in_specs=in_specs, out_specs=out_specs
        ),
        out_shape=out_shape,
        compiler_params=pltpu.CompilerParams(vmem_limit_bytes=VMEM),
        cost_estimate=SHORT,
    )(place, *args)
    return out if norms is not None else out[0]


def forward_kernel(rows_ref, mine_ref, other_ref, bias_ref, act_ref, slope_ref):
    half = mine_ref.shape[0]
    step = 256
    for start in range(0, rows_ref.shape[0], step):
        at = slice(start, start + step)
        h = jnp.dot(rows_ref[at, :half], mine_ref[...], preferred_element_type=f32)
        h += jnp.dot(rows_ref[at, half:], other_ref[...], preferred_element_type=f32)
        act, slope = gelu_and_slope(h + bias_ref[...].astype(f32))
        act_ref[at, :] = act.astype(bf16)
        slope_ref[at, :] = slope.astype(bf16)


def backward_kernel(rows_ref, mine_ref, other_ref, slope_ref, grad_ref, sum_ref):
    half = mine_ref.shape[0]
    step = 256
    total = jnp.zeros(sum_ref.shape, f32)
    for start in range(0, rows_ref.shape[0], step):
        at = slice(start, start + step)
        h = jnp.dot(rows_ref[at, :half], mine_ref[...], preferred_element_type=f32)
        h += jnp.dot(rows_ref[at, half:], other_ref[...], preferred_element_type=f32)
        h *= slope_ref[at, :].astype(f32)
        grad_ref[at, :] = h.astype(bf16)
        total += jnp.sum(h, axis=0, keepdims=True)
    sum_ref[...] = total


def hidden_layer(kernel, rows, weight, last, outs):
    mine, other = weight
    count, depth = rows.shape
    cols = mine.shape[1]
    tile = COLUMNS

    def spec(height):
        return pl.BlockSpec((height, tile), lambda i: (0, i))

    return pl.pallas_call(
        kernel,
        grid=(cols // tile,),
        in_specs=[
            pl.BlockSpec((count, depth), lambda i: (0, 0)),
            spec(depth // 2),
            spec(depth // 2),
            spec(last.shape[0]),
        ],
        out_specs=[spec(o.shape[0]) for o in outs],
        out_shape=outs,
        compiler_params=pltpu.CompilerParams(vmem_limit_bytes=VMEM),
        cost_estimate=SHORT,
    )(rows, mine, other, last)


def rotary_tables(length, lanes):
    half_rot = ROT // 2
    freqs = jnp.exp(jnp.arange(half_rot, dtype=f32) * (-2.0 * math.log(10000.0) / ROT))
    angles = jnp.arange(length, dtype=jnp.int32).astype(f32)[:, None] * freqs[None, :]
    cosine = jnp.cos(angles)
    sine = jnp.sin(angles)
    zero = jnp.zeros((length, half_rot), f32)
    rest_one = jnp.ones((length, HD - ROT), f32)
    rest_zero = jnp.zeros((length, HD - ROT), f32)
    keep = jnp.concatenate([cosine, cosine, rest_one], -1)
    from_high = jnp.concatenate([-sine, zero, rest_zero], -1)
    from_low = jnp.concatenate([zero, sine, rest_zero], -1)
    many = lanes // HD
    return jnp.stack([jnp.tile(v, (1, many)) for v in (keep, from_high, from_low)])


def attention_kernel(
    tile, slot_ref, q_ref, k_ref, v_ref, grad_ref, table_ref, attn_ref, dproj_ref, bias_ref, *scratch
):
    q_s, k_s, v_s, g_s, qt_s, kt_s, vt_s, gt_s, at_s, dqt_s, dk_s, dv_s = scratch
    length, lanes = q_ref.shape
    blocks = slot_ref.shape[0]
    block = length // blocks
    tiles = length // tile
    half_rot = ROT // 2
    scale = HD ** (-0.5)
    many = lanes // HD
    width = dproj_ref.shape[1] // 3

    def turn(u, at, sign):
        keep, high, low = table_ref[0, at, :], table_ref[1, at, :], table_ref[2, at, :]
        moved = pltpu.roll(u, lanes - half_rot, 1) * high + pltpu.roll(u, half_rot, 1) * low
        return u * keep + sign * moved

    def places(b):
        at = slice(b * block, (b + 1) * block)
        return at, pl.ds(pl.multiple_of(slot_ref[b] * block, block), block)

    for b in range(blocks):
        at, came = places(b)
        q = turn(q_ref[came, :], at, 1.0).astype(bf16).astype(f32) * scale
        k = turn(k_ref[came, :], at, 1.0).astype(bf16).astype(f32)
        v = v_ref[came, :].astype(bf16).astype(f32)
        g = grad_ref[came, :].astype(f32)
        for value, flat, turned in ((q, q_s, qt_s), (k, k_s, kt_s), (v, v_s, vt_s), (g, g_s, gt_s)):
            turned[:, at] = value.T.astype(bf16)
            for h in range(many):
                flat[h, at, :] = value[:, h * HD : (h + 1) * HD].astype(bf16)

    row = lax.broadcasted_iota(jnp.int32, (tile, tile), 0)
    col = lax.broadcasted_iota(jnp.int32, (tile, tile), 1)
    hidden = row > col

    def mm(a, b):
        return jnp.dot(a, b, preferred_element_type=f32)

    for h in range(many):
        feats = slice(h * HD, (h + 1) * HD)
        for i in range(tiles):
            qs = slice(i * tile, (i + 1) * tile)
            q_t = qt_s[feats, qs]
            scores = []
            for j in range(i + 1):
                s = mm(k_s[h, j * tile : (j + 1) * tile, :], q_t)
                scores.append(jnp.where(hidden, NEG_BIG, s) if j == i else s)
            top = functools.reduce(
                jnp.maximum, [jnp.max(s, axis=0, keepdims=True) for s in scores]
            )
            weights = [jnp.exp(s - top) for s in scores]
            total = functools.reduce(
                jnp.add, [jnp.sum(w, axis=0, keepdims=True) for w in weights]
            )
            mixed = functools.reduce(
                jnp.add,
                [
                    mm(vt_s[feats, j * tile : (j + 1) * tile], w.astype(bf16))
                    for j, w in enumerate(weights)
                ],
            )
            mixed = (mixed / total).astype(bf16).astype(f32)
            at_s[feats, qs] = mixed
            g_t = gt_s[feats, qs]
            delta = jnp.sum(g_t.astype(f32) * mixed, axis=0, keepdims=True)
            inverse = 1.0 / total
            dq = None
            for j in range(i + 1):
                ks = slice(j * tile, (j + 1) * tile)
                p = weights[j] * inverse
                dp = mm(v_s[h, ks, :], g_t)
                ds = (p * (dp - delta)).astype(bf16)
                dv = mm(p.astype(bf16), g_s[h, qs, :])
                dk = mm(ds, q_s[h, qs, :])
                if i == j:
                    dv_s[h, ks, :] = dv
                    dk_s[h, ks, :] = dk
                else:
                    dv_s[h, ks, :] += dv
                    dk_s[h, ks, :] += dk
                part = mm(kt_s[feats, ks], ds)
                dq = part if dq is None else dq + part
            dqt_s[feats, qs] = dq * scale

    sums = [jnp.zeros((1, lanes), f32) for _ in range(3)]
    for b in range(blocks):
        at, came = places(b)
        attn_ref[came, :] = at_s[:, at].T.astype(bf16)
        dq = turn(dqt_s[:, at].T, at, -1.0)
        dk = turn(jnp.concatenate([dk_s[h, at, :] for h in range(many)], 1), at, -1.0)
        dv = jnp.concatenate([dv_s[h, at, :] for h in range(many)], 1)
        for index, value in enumerate((dq, dk, dv)):
            lane = pl.multiple_of(index * width + pl.program_id(1) * lanes, lanes)
            dproj_ref[came, pl.ds(lane, lanes)] = value.astype(bf16)
            sums[index] = sums[index] + jnp.sum(value, axis=0, keepdims=True)
    for index in range(3):
        bias_ref[0, index] = sums[index]


def attention_whole(proj, attn_grad, plan, tables):
    rows = proj.shape[0]
    width = proj.shape[1] // 3
    per, members = plan.per, plan.members
    length = rows // per
    tile = min(256, length)
    many = LANES // HD
    steps = width // LANES
    slots = jnp.sum(
        jnp.where(
            plan.order[None, :] == jnp.arange(members, dtype=jnp.int32)[:, None],
            jnp.arange(members, dtype=jnp.int32)[None, :],
            0,
        ),
        axis=1,
    ).astype(jnp.int32)
    flat = pltpu.VMEM((many, length, HD), bf16)
    turned = pltpu.VMEM((LANES, length), bf16)
    wide = pltpu.VMEM((LANES, length), f32)
    sums = pltpu.VMEM((many, length, HD), f32)

    def columns(part):
        return pl.BlockSpec((length, LANES), lambda s, h, o: (s, part * steps + h))

    attn, dproj, bias = pl.pallas_call(
        functools.partial(attention_kernel, tile),
        grid_spec=pltpu.PrefetchScalarGridSpec(
            num_scalar_prefetch=1,
            grid=(per, steps),
            in_specs=[
                columns(0),
                columns(1),
                columns(2),
                columns(0),
                pl.BlockSpec((3, length, LANES), lambda s, h, o: (0, 0, 0)),
            ],
            out_specs=[
                columns(0),
                pl.BlockSpec((length, 3 * width), lambda s, h, o: (s, 0)),
                pl.BlockSpec((1, 3, 1, LANES), lambda s, h, o: (s, 0, 0, h)),
            ],
            scratch_shapes=[flat] * 4 + [turned] * 4 + [wide] * 2 + [sums] * 2,
        ),
        out_shape=[
            jax.ShapeDtypeStruct((rows, width), bf16),
            jax.ShapeDtypeStruct((rows, 3 * width), bf16),
            jax.ShapeDtypeStruct((per, 3, 1, width), f32),
        ],
        compiler_params=pltpu.CompilerParams(vmem_limit_bytes=VMEM),
        cost_estimate=SHORT,
    )(slots, proj, proj, proj, attn_grad, tables)
    return attn, dproj, jnp.sum(bias, axis=(0, 2)).reshape(-1)


def rotate(values, cosine, sine):
    half_rot = ROT // 2
    front = values[..., :ROT]
    turned = jnp.concatenate([-front[..., half_rot:], front[..., :half_rot]], -1)
    return jnp.concatenate([front * cosine + turned * sine, values[..., ROT:]], -1)


def rotate_back(grads, cosine, sine):
    half_rot = ROT // 2
    front = grads[..., :ROT]
    by_sine = front * sine
    turned = jnp.concatenate([by_sine[..., half_rot:], -by_sine[..., :half_rot]], -1)
    return jnp.concatenate([front * cosine + turned, grads[..., ROT:]], -1)


def attention_split(proj, attn_grad, plan, block_len):
    rows = attn_grad.shape[0]
    width = attn_grad.shape[1]
    per, members, groups = plan.per, plan.members, plan.groups
    count = rows // per
    heads = width // HD

    def positions(blocks):
        inside = jnp.arange(block_len, dtype=jnp.int32)
        return (blocks[:, None] * block_len + inside[None, :]).reshape(-1)

    position = positions(plan.order)
    every = positions(plan.all_order)
    half_rot = ROT // 2
    freqs = jnp.exp(jnp.arange(half_rot, dtype=f32) * (-2.0 * math.log(10000.0) / ROT))
    angles = position.astype(f32)[:, None] * freqs[None, :]
    cosine = jnp.concatenate([jnp.cos(angles)] * 2, -1)[None, :, None, :]
    sine = jnp.concatenate([jnp.sin(angles)] * 2, -1)[None, :, None, :]
    teams = [[m + members * g for g in range(groups)] for m in range(members)]

    def team_gather(value, axis):
        return lax.all_gather(
            value, "context", axis=axis, tiled=True, axis_index_groups=teams
        )

    def team_sum(value):
        return lax.psum_scatter(
            value, "context", scatter_dimension=1, tiled=True, axis_index_groups=teams
        )

    shape = (per, count, heads, HD)
    q = rotate(proj[:, :width].reshape(shape), cosine, sine).astype(bf16)
    k = rotate(proj[:, width : 2 * width].reshape(shape), cosine, sine).astype(bf16)
    v = proj[:, 2 * width :].reshape(shape).astype(bf16)
    g = attn_grad.reshape(shape)
    k_all = team_gather(k, 1)
    v_all = team_gather(v, 1)
    visible = every[None, :] <= position[:, None]
    scale = HD ** (-0.5)
    outs, dqs, dks, dvs = [], [], [], []
    for h in range(heads):
        s = dot("sqd,skd->sqk", q[:, :, h], k_all[:, :, h]) * scale
        s = jnp.where(visible, s, NEG_BIG)
        top = jnp.max(s, -1, keepdims=True)
        e = jnp.where(visible, jnp.exp(s - top), 0.0)
        total = jnp.sum(e, -1, keepdims=True)
        o = (dot("sqk,skd->sqd", e.astype(bf16), v_all[:, :, h]) / total).astype(bf16)
        delta = jnp.sum(g[:, :, h].astype(f32) * o.astype(f32), -1, keepdims=True)
        p = e / total
        dp = dot("sqd,skd->sqk", g[:, :, h], v_all[:, :, h])
        ds = (p * (dp - delta) * scale).astype(bf16)
        outs.append(o)
        dqs.append(dot("sqk,skd->sqd", ds, k_all[:, :, h]))
        dks.append(dot("sqk,sqd->skd", ds, q[:, :, h]))
        dvs.append(dot("sqk,sqd->skd", p.astype(bf16), g[:, :, h]))
    attn = jnp.concatenate(outs, -1).reshape(rows, width)
    dq = rotate_back(jnp.stack(dqs, 2), cosine, sine).reshape(rows, width)
    dk = team_sum(jnp.concatenate(dks, -1)).reshape(shape)
    dk = rotate_back(dk, cosine, sine).reshape(rows, width)
    dv = team_sum(jnp.concatenate(dvs, -1)).reshape(rows, width)
    dproj = jnp.concatenate([dq, dk, dv], -1)
    return attn, dproj.astype(bf16), jnp.sum(dproj, axis=0)


def general_block(
    block_in,
    norm_gain,
    layer_norm_bias,
    qkv_weight,
    qkv_bias,
    out_weight,
    out_bias,
    fc1_weight,
    fc1_bias,
    fc2_weight,
    fc2_bias,
    block_order,
    out_grad,
):
    seq_count, block_len, width = block_in.shape
    plan = Rows(seq_count, block_order)
    x_own = plan.gather(block_in)
    g_own = plan.gather(out_grad)
    qkv_flat = qkv_weight.swapaxes(0, 1).reshape(qkv_weight.shape[1], -1)
    qkv_full = lax.all_gather(qkv_flat, "context", axis=0, tiled=True)
    out_full = lax.all_gather(out_weight, "context", axis=1, tiled=True)
    fc1_full = lax.all_gather(fc1_weight, "context", axis=0, tiled=True)
    fc2_full = lax.all_gather(fc2_weight, "context", axis=1, tiled=True)
    x_full, g_full, gain, shift = (
        lax.all_gather(v, "tensor", axis=v.ndim - 1, tiled=True)
        for v in (x_own, g_own, norm_gain, layer_norm_bias)
    )
    centred = x_full.astype(f32)
    mean = jnp.mean(centred, -1, keepdims=True)
    centred = centred - mean
    inv_std = lax.rsqrt(jnp.mean(centred * centred, -1, keepdims=True) + NORM_EPS)
    xhat = centred * inv_std
    normed = (xhat * gain.astype(f32) + shift.astype(f32)).astype(bf16)

    proj = dot("rd,de->re", normed, qkv_full) + qkv_bias.astype(f32).reshape(-1)
    attn_grad = dot("rd,ed->re", g_full, out_full).astype(bf16)
    if plan.groups == 1:
        tables = rotary_tables(proj.shape[0] // plan.per, LANES)
        attn, dproj, qkvb_sum = attention_whole(proj, attn_grad, plan, tables)
    else:
        attn, dproj, qkvb_sum = attention_split(proj, attn_grad, plan, block_len)
    hidden_pre = dot("rd,df->rf", normed, fc1_full) + fc1_bias.astype(f32)
    hidden_act, slope = gelu_and_slope(hidden_pre)
    hidden_act = hidden_act.astype(bf16)
    hidden_grad = dot("rd,fd->rf", g_full, fc2_full) * slope
    fc1b_sum = jnp.sum(hidden_grad, axis=0)
    hidden_grad = hidden_grad.astype(bf16)

    def rows_summed(part):
        part = part.astype(bf16)
        return lax.psum_scatter(part, "context", scatter_dimension=0, tiled=True).astype(f32)

    qkv_w_g = rows_summed(dot("rd,re->de", normed, dproj))
    out_w_g = rows_summed(dot("rd,re->de", g_full, attn))
    fc2_w_g = rows_summed(dot("rd,rf->df", g_full, hidden_act))
    fc1_w_g = rows_summed(dot("rd,rf->df", normed, hidden_grad))

    def features_summed(value):
        value = value.astype(bf16)
        return lax.psum_scatter(value, "tensor", scatter_dimension=1, tiled=True).astype(f32)

    part = dot("re,de->rd", dproj, qkv_full) + dot("rf,df->rd", hidden_grad, fc1_full)
    scaled = part * gain.astype(f32)
    row_sums = jnp.stack([jnp.sum(scaled, -1), jnp.sum(scaled * xhat, -1)])
    row_sums = sum_over(row_sums, "tensor")
    norm_own = features_summed(part)
    branch = features_summed(
        dot("re,ed->rd", attn, out_full) + dot("rf,fd->rd", hidden_act, fc2_full)
    )
    change, sums = row_change(x_own, mean, inv_std, row_sums, norm_own, norm_gain)
    return finish(
        (block_in, out_grad, out_bias, fc2_bias, qkv_bias),
        (plan.scatter(change), plan.scatter(branch.astype(bf16))),
        (qkvb_sum, fc1b_sum, *sums),
        (jnp.concatenate([qkv_w_g, out_w_g], 1), 3 * width, fc1_w_g, fc2_w_g),
    )


def row_change(x_own, mean, inv_std, row_sums, norm_own, norm_gain):
    xhat_own = (x_own.astype(f32) - mean) * inv_std
    row_means = row_sums / (x_own.shape[1] * lax.axis_size("tensor"))
    change = inv_std * (
        norm_own * norm_gain.astype(f32)
        - row_means[0][:, None]
        - xhat_own * row_means[1][:, None]
    )
    sums = jnp.sum(norm_own * xhat_own, axis=0), jnp.sum(norm_own, axis=0)
    return change.astype(bf16), sums


def finish(given, rows, bias_sums, weights):
    block_in, out_grad, out_bias, fc2_bias, qkv_bias = given
    change, branch = rows
    qkvb_sum, fc1b_sum, gain_sum, beta_sum = bias_sums
    attn_w_g, qkv_width, fc1_w_g, fc2_w_g = weights
    width = block_in.shape[-1]
    block_out = (
        block_in.astype(f32)
        + branch.astype(f32)
        + out_bias.astype(f32)
        + fc2_bias.astype(f32)
    ).astype(bf16)
    grad_own = out_grad.astype(f32)
    input_grad = grad_own + change.astype(f32)

    outb_sum = jnp.sum(grad_own, axis=(0, 1))
    sums = (qkvb_sum, outb_sum, fc1b_sum, gain_sum, beta_sum)
    joined = sum_over(jnp.concatenate(sums), "context")
    cuts = []
    start = 0
    for part in sums:
        cuts.append(joined[start : start + part.shape[0]])
        start += part.shape[0]
    qkv_b_g, outb_g, fc1_b_g, gain_g, beta_g = cuts
    return (
        block_out,
        input_grad,
        gain_g,
        beta_g,
        attn_w_g[:, :qkv_width].reshape(-1, 3, width).swapaxes(0, 1),
        qkv_b_g.reshape(qkv_bias.shape),
        attn_w_g[:, qkv_width:].T,
        outb_g,
        fc1_w_g,
        fc1_b_g,
        fc2_w_g.T,
        outb_g,
    )


def staged_block(
    block_in,
    norm_gain,
    layer_norm_bias,
    qkv_weight,
    qkv_bias,
    out_weight,
    out_bias,
    fc1_weight,
    fc1_bias,
    fc2_weight,
    fc2_bias,
    block_order,
    out_grad,
):
    seq_count, block_len, width = block_in.shape
    plan = Rows(seq_count, block_order)
    ctx = lax.axis_index("context")
    z, k = ctx // 2, ctx % 2
    ten = lax.axis_index("tensor")
    qkv_width = 3 * width

    norm_pieces = neighbours(jnp.stack([norm_gain, layer_norm_bias]))
    x_own = plan.gather(block_in)
    first = jnp.concatenate(
        [qkv_weight.swapaxes(0, 1).reshape(qkv_weight.shape[1], -1), out_weight.T], 1
    )
    fc2_own = fc2_weight.T
    tables = rotary_tables(plan.members * block_len, LANES)
    x_own, norm_pieces, first, fc2_own, grad_in, tables = fence(
        x_own, norm_pieces, first, fc2_own, out_grad, tables
    )
    first_full = lax.all_gather(first, "context", axis=0, tiled=True)
    g_own = plan.gather(grad_in)
    near = [swap(x_own, "tensor", m) for m in (1, 2)]
    spread = Spread(fc1_weight, fc2_own)
    x_pieces, g_own, spread.own = fence(far_pieces(x_own, near), g_own, spread.own)
    spread.step()
    near = [swap(g_own, "tensor", m) for m in (1, 2)]
    gains = jnp.stack([p[0] for p in norm_pieces])
    shifts = jnp.stack([p[1] for p in norm_pieces])
    g_pieces = far_pieces(g_own, near)
    normed, normed_c, normed_t, normed_o, mean, inv_std = join_features(
        x_pieces, gains, shifts
    )
    g_full, g_c, g_t, g_o = join_features(g_pieces)
    first_full, normed, normed_c, normed_t, normed_o, g_full, g_c, g_t, g_o = fence(
        first_full, normed, normed_c, normed_t, normed_o, g_full, g_c, g_t, g_o
    )
    first_full, spread.got = fence(first_full, spread.got)
    qkv_full = first_full[:, :qkv_width]
    out_full = first_full[:, qkv_width:]

    spread.step()
    normed_o, g_o = swap(normed_o, "context", 1), swap(g_o, "context", 1)
    proj = dot("rd,de->re", normed, qkv_full) + qkv_bias.astype(f32).reshape(-1)
    attn_grad = dot("rd,de->re", g_full, out_full).astype(bf16)
    attn, dproj, qkvb_sum = attention_whole(proj, attn_grad, plan, tables)
    spread.got, attn, dproj, normed_o, g_o = fence(spread.got, attn, dproj, normed_o, g_o)

    spread.step()
    attn_sum = ChainSum(
        (normed_t, dproj, normed_o, swap(dproj, "context", 1)),
        (g_t, attn, g_o, swap(attn, "context", 1)),
    )
    (attn_sum.held,) = fence(attn_sum.held)

    attn_sum.step()
    spread.got, attn_sum.held = fence(spread.got, attn_sum.held)

    fc1_mine, sends = fence(spread.joined(0), attn_sum.ready())
    attn_sum.step(sends)
    fc1_full = fc1_mine, swap(fc1_mine, "context", 1)
    (fc1_full,) = fence(fc1_full)

    wide = jax.ShapeDtypeStruct((normed_c.shape[0], fc1_bias.shape[0]), bf16)
    hidden_act, slope = hidden_layer(
        forward_kernel, normed_c, fc1_full, fc1_bias.reshape(1, -1), [wide, wide]
    )
    spread.got, hidden_act, slope, attn_sum.held = fence(
        spread.got, hidden_act, slope, attn_sum.held
    )

    hidden_o = swap(hidden_act, "context", 1)
    fc2_mine, hidden_o, sends = fence(spread.joined(1), hidden_o, attn_sum.ready())
    attn_sum.step(sends)
    fc2_full = fc2_mine, swap(fc2_mine, "context", 1)
    fc2_sum = ChainSum((g_t, hidden_act, g_o, hidden_o))
    fc2_full, fc2_sum.held, attn_sum.held = fence(fc2_full, fc2_sum.held, attn_sum.held)

    fc2_sum.step()
    line = jax.ShapeDtypeStruct((1, fc1_bias.shape[0]), f32)
    hidden_grad, fc1b_sum = hidden_layer(
        backward_kernel, g_c, fc2_full, slope, [wide, line]
    )
    fc1b_sum = fc1b_sum.reshape(-1)
    fc2_sum.held, hidden_grad, attn = fence(fc2_sum.held, hidden_grad, attn)

    masks = jnp.arange(3, -1, -1, dtype=jnp.int32)
    owners = ten.astype(jnp.int32) ^ masks
    place = jnp.concatenate([owners, (z - owners) & 3, k.reshape(1)]).astype(jnp.int32)
    fc2_sum.step()
    hidden_grad_o = swap(hidden_grad, "context", 1)
    chunks = feature_chunks(place, attn, hidden_act, first_full, qkv_width, fc2_full)
    fc2_sum.held, hidden_grad_o, chunks = fence(fc2_sum.held, hidden_grad_o, chunks)

    fc2_sum.step()
    branch_sum = FeatureSum(chunks)
    fc1_sum = ChainSum((normed_t, hidden_grad, normed_o, hidden_grad_o))
    fc2_sum.held, branch_sum.held, fc1_sum.held, dproj = fence(
        fc2_sum.held, branch_sum.held, fc1_sum.held, dproj
    )

    fc1_sum.step()
    branch_sum.step()
    norm_chunks, row_sums = feature_chunks(
        place, dproj, hidden_grad, first_full, 0, fc1_full, (gains, shifts, normed)
    )
    fc1_sum.held, branch_sum.held, norm_chunks, row_sums = fence(
        fc1_sum.held, branch_sum.held, norm_chunks, row_sums
    )

    sends = fc1_sum.ready()
    branch = branch_sum.total().astype(bf16)
    sends, branch, norm_chunks, row_sums = fence(sends, branch, norm_chunks, row_sums)
    fc1_sum.step(sends)
    norm_sum = FeatureSum(norm_chunks)
    branch = plan.scatter(branch)
    row_sums = sum(neighbours(row_sums[..., 0]))
    attn_w_g = attn_sum.total()
    norm_sum.held, row_sums, attn_w_g = fence(norm_sum.held, row_sums, attn_w_g)
    norm_sum.step()
    fc2_w_g = fc2_sum.total()
    fc1_sum.held, norm_sum.held, fc2_w_g = fence(fc1_sum.held, norm_sum.held, fc2_w_g)

    sends = fc1_sum.ready()
    change, sums = row_change(x_own, mean, inv_std, row_sums, norm_sum.total(), norm_gain)
    sends, change, branch = fence(sends, change, branch)
    fc1_sum.step(sends)
    change = plan.scatter(change)
    return finish(
        (block_in, out_grad, out_bias, fc2_bias, qkv_bias),
        (change, branch),
        (qkvb_sum, fc1b_sum, *sums),
        (attn_w_g, qkv_width, fc1_sum.total(), fc2_w_g),
    )


def on_device(*args):
    block_in, block_order = args[0], args[11]
    four = lax.axis_size("context") == 8 and lax.axis_size("tensor") == 4
    if four and block_in.shape[0] % 8 == 0:
        return staged_block(*args)
    return general_block(*args)


def solution(mesh):
    rows = P(None, "context", "tensor")
    in_specs = (
        rows,
        P("tensor"),
        P("tensor"),
        P(None, "context", "tensor"),
        P(None, "tensor"),
        P("tensor", "context"),
        P("tensor"),
        P("context", "tensor"),
        P("tensor"),
        P("tensor", "context"),
        P("tensor"),
        P(),
        rows,
    )
    out_specs = (
        rows,
        rows,
        P("tensor"),
        P("tensor"),
        P(None, "context", "tensor"),
        P(None, "tensor"),
        P("tensor", "context"),
        P("tensor"),
        P("context", "tensor"),
        P("tensor"),
        P("tensor", "context"),
        P("tensor"),
    )
    return jax.shard_map(
        on_device, mesh=mesh, in_specs=in_specs, out_specs=out_specs, check_vma=False
    )
```

```python
import functools
import math

import jax
import jax.numpy as jnp
from jax import lax
from jax.experimental import pallas as pl
from jax.experimental.pallas import tpu as pltpu
from jax.sharding import PartitionSpec as P

HD = 64
ROT = 32

NORM_EPS = 1e-05
NEG_BIG = -1e30
GELU_COEF = 0.7978845608028654
GELU_CUBE = 0.044715

LANES = 128
VMEM = 60 * 1024 * 1024

f32 = jnp.float32
bf16 = jnp.bfloat16


def dot(spec, a, b):
    return jnp.einsum(spec, a, b, preferred_element_type=f32)


def gelu_and_slope(h):
    t = jnp.tanh(GELU_COEF * (h + GELU_CUBE * h * h * h))
    act = 0.5 * h * (1.0 + t)
    slope = 0.5 * (1.0 + t) + 0.5 * h * (1.0 - t * t) * GELU_COEF * (
        1.0 + 3.0 * GELU_CUBE * h * h
    )
    return act, slope


def swap(value, axis, mask):
    size = lax.axis_size(axis)
    return lax.ppermute(value, axis, [(i, i ^ mask) for i in range(size)])


def sum_over(value, axis):
    size = lax.axis_size(axis)
    if size & (size - 1):
        return lax.psum(value, axis)
    mask = 1
    while mask < size:
        value = value + swap(value, axis, mask)
        mask *= 2
    return value


def fence(*values):
    return lax.optimization_barrier(values)


class Rows:
    def __init__(self, seq_count, block_order):
        n_ctx = lax.axis_size("context")
        self.members = math.gcd(seq_count, n_ctx)
        self.groups = n_ctx // self.members
        self.per = seq_count // self.members
        self.all_order = block_order
        start = lax.axis_index("context") // self.members * self.members
        self.order = lax.dynamic_slice_in_dim(block_order, start, self.members)

    def _exchange(self, split):
        teams = None
        if self.groups > 1:
            teams = [
                [g * self.members + m for m in range(self.members)] for g in range(self.groups)
            ]
        return lax.all_to_all(split, "context", 0, 0, axis_index_groups=teams, tiled=True)

    def gather(self, rows):
        seqs, block, width = rows.shape
        got = self._exchange(rows.reshape(self.members, self.per, block, width))
        return got.swapaxes(0, 1).reshape(self.per * self.members * block, width)

    def scatter(self, rows):
        width = rows.shape[-1]
        split = rows.reshape(self.per, self.members, -1, width).swapaxes(0, 1)
        got = self._exchange(split)
        return got.reshape(self.members * self.per, split.shape[2], width)


def neighbours(small):
    return [small] + [swap(small, "tensor", m) for m in range(1, lax.axis_size("tensor"))]


def far_pieces(rows, near):
    half = rows.shape[0] // 2
    near_x, near_y = near
    far_top = swap(near_y[:half], "tensor", 1)
    far_low = swap(near_x[half:], "tensor", 2)
    return rows, near_x, near_y, far_top, far_low


def joined_kernel(place_ref, own, near_x, near_y, far_top, far_low, *rest):
    normed = len(rest) > 4
    width = own.shape[1]
    top = pl.program_id(0) < pl.num_programs(0) // 2
    far = jnp.where(top, far_top[...].astype(f32), far_low[...].astype(f32))
    pieces = [own[...].astype(f32), near_x[...].astype(f32), near_y[...].astype(f32), far]
    if normed:
        gain_ref, shift_ref, out_ref, out_c_ref, out_t_ref, out_o_ref = rest[:6]
        mean_ref, inv_ref = rest[6:]
        total = 4 * width
        mean = sum(jnp.sum(p, -1, keepdims=True) for p in pieces) / total
        centred = [p - mean for p in pieces]
        spread = sum(jnp.sum(c * c, -1, keepdims=True) for c in centred) / total
        inv = lax.rsqrt(spread + NORM_EPS)
        mean_ref[...] = mean
        inv_ref[...] = inv
        pieces = [
            c * inv * gain_ref[m : m + 1].astype(f32) + shift_ref[m : m + 1].astype(f32)
            for m, c in enumerate(centred)
        ]
    else:
        out_ref, out_c_ref, out_t_ref, out_o_ref = rest
    half = width // 2
    for m, piece in enumerate(pieces):
        owner = place_ref[0] ^ m
        out_ref[:, pl.ds(pl.multiple_of(owner * width, LANES), width)] = piece.astype(bf16)
        for c in range(2):
            slot = (place_ref[2] - owner) & 3
            at = pl.ds(pl.multiple_of(slot * half, LANES), half)
            side = place_ref[1] ^ c
            wide = pl.ds(pl.multiple_of((side * 4 + slot) * half, LANES), half)
            part = piece[:, c * half : (c + 1) * half]
            out_c_ref[:, wide] = part.astype(bf16)
            turned = part.T.astype(bf16)

            @pl.when(side == 0)
            def _(at=at, turned=turned):
                out_t_ref[at, :] = turned

            @pl.when(side == 1)
            def _(at=at, turned=turned):
                out_o_ref[at, :] = turned


def join_features(pieces, gains=None, shifts=None):
    rows, width = pieces[0].shape
    block = min(128, rows // 2)
    steps = rows // block
    ctx = lax.axis_index("context")
    place = jnp.stack([lax.axis_index("tensor"), ctx % 2, ctx // 2]).astype(jnp.int32)
    piece = pl.BlockSpec((block, width), lambda i, t: (i, 0))
    top = pl.BlockSpec((block, width), lambda i, t: (jnp.minimum(i, steps // 2 - 1), 0))
    low = pl.BlockSpec((block, width), lambda i, t: (jnp.maximum(i - steps // 2, 0), 0))
    in_specs = [piece] * 3 + [top, low]
    args = list(pieces)
    out_specs = [pl.BlockSpec((block, 4 * width), lambda i, t: (i, 0))] * 2
    out_specs += [pl.BlockSpec((2 * width, block), lambda i, t: (0, i))] * 2
    out_shape = [jax.ShapeDtypeStruct((rows, 4 * width), bf16)] * 2
    out_shape += [jax.ShapeDtypeStruct((2 * width, rows), bf16)] * 2
    if gains is not None:
        in_specs += [pl.BlockSpec((4, width), lambda i, t: (0, 0))] * 2
        args += [gains, shifts]
        out_specs += [pl.BlockSpec((block, 1), lambda i, t: (i, 0))] * 2
        out_shape += [jax.ShapeDtypeStruct((rows, 1), f32)] * 2
    out = pl.pallas_call(
        joined_kernel,
        grid_spec=pltpu.PrefetchScalarGridSpec(
            num_scalar_prefetch=1, grid=(steps,), in_specs=in_specs, out_specs=out_specs
        ),
        out_shape=out_shape,
        compiler_params=pltpu.CompilerParams(vmem_limit_bytes=VMEM),
        cost_estimate=pl.CostEstimate(
            flops=40 * rows * width, bytes_accessed=16 * rows * width, transcendentals=rows
        ),
    )(place, *args)
    return out


class FeatureSum:
    def __init__(self, chunks):
        self.chunks = chunks
        half = chunks.shape[1] // 2
        self.held = (
            swap(chunks[0, :half], "tensor", 1),
            swap(chunks[0, half:], "tensor", 2),
        )

    def step(self):
        via_x, via_y = self.held
        half = via_x.shape[0]

        def joined(value, via, top):
            ends = [value[:half].astype(f32), value[half:].astype(f32)]
            ends[0 if top else 1] += via.astype(f32)
            return jnp.concatenate(ends, 0).astype(bf16)

        from_y = swap(joined(self.chunks[1], via_x, True), "tensor", 2)
        from_x = swap(joined(self.chunks[2], via_y, False), "tensor", 1)
        self.held = from_x, from_y

    def total(self):
        from_x, from_y = self.held
        return self.chunks[3].astype(f32) + from_x.astype(f32) + from_y.astype(f32)


def hop(value, by, low, high):
    table = [(2 * i + c, 2 * (i + by) + c) for i in range(low, high + 1) for c in range(2)]
    return lax.ppermute(value, "context", table)


def merge_kernel(own_ref, *refs):
    out = refs[-1]
    part = own_ref.shape[1]
    out[:part, :] = own_ref[0]
    for slot in range(3):
        at = slice((slot + 1) * part, (slot + 2) * part)
        out[at, :] = refs[2 * slot][0] + refs[2 * slot + 1][0]


class Spread:
    def __init__(self, *own):
        self.own = jnp.stack(own)
        self.got = []

    def step(self):
        n = len(self.got)
        up, down = self.got[-1] if n else (self.own, self.own)
        self.got = self.got + [(hop(up, 1, n, 2), hop(down, -1, 1, 3 - n))]

    def joined(self, n):
        (up1, down1), (up2, down2), (up3, down3) = self.got
        _, part, cols = self.own.shape
        return pl.pallas_call(
            merge_kernel,
            grid=(cols // COLUMNS,),
            in_specs=[pl.BlockSpec((1, part, COLUMNS), lambda i: (n, 0, i))] * 7,
            out_specs=pl.BlockSpec((4 * part, COLUMNS), lambda i: (0, i)),
            out_shape=jax.ShapeDtypeStruct((4 * part, cols), bf16),
            compiler_params=pltpu.CompilerParams(vmem_limit_bytes=VMEM),
            cost_estimate=SHORT,
        )(self.own, up1, down3, up2, down2, up3, down1)


SHORT = pl.CostEstimate(flops=1, bytes_accessed=4 * 1024 * 1024, transcendentals=0)
COLUMNS = 512


def grad_kernel(tiles, *refs):
    given, outs = refs[: 4 * len(tiles)], refs[4 * len(tiles) :]
    part = outs[0].shape[0]
    first = 0
    for n, count in enumerate(tiles):
        own_ref, own_values, other_ref, other_values = given[4 * n : 4 * n + 4]
        step = pl.program_id(0)

        @pl.when((step >= first) & (step < first + count))
        def _(own=own_ref, own_v=own_values, other=other_ref, other_v=other_values):
            for slot in range(4):
                at = slice(slot * part, (slot + 1) * part)
                total = jnp.dot(own[at, :], own_v[...], preferred_element_type=f32)
                total += jnp.dot(other[at, :], other_v[...], preferred_element_type=f32)
                outs[slot][...] = total.astype(bf16)

        first += count


class ChainSum:
    def __init__(self, *products):
        half, count = products[0][2].shape
        tiles = [p[1].shape[1] // COLUMNS for p in products]
        in_specs, first = [], 0
        for number in tiles:
            rows = pl.BlockSpec((half, count), lambda i: (0, 0))
            values = pl.BlockSpec(
                (count, COLUMNS),
                lambda i, first=first, last=number - 1: (0, jnp.clip(i - first, 0, last)),
            )
            in_specs += [rows, values] * 2
            first += number
        moving = pl.BlockSpec((half // 4, COLUMNS), lambda i: (0, i))
        shape = jax.ShapeDtypeStruct((half // 4, first * COLUMNS), bf16)
        parts = pl.pallas_call(
            functools.partial(grad_kernel, tiles),
            grid=(first,),
            in_specs=in_specs,
            out_specs=[moving] * 4,
            out_shape=[shape] * 4,
            compiler_params=pltpu.CompilerParams(vmem_limit_bytes=VMEM),
            cost_estimate=SHORT,
        )(*(v for p in products for v in p))
        self.held = parts, ()

    def ready(self):
        parts, before = self.held
        n = len(before)
        up, down = parts[n + 1], parts[3 - n]
        if n:
            last_up, last_down = before[-1]
            up = (up.astype(f32) + last_up.astype(f32)).astype(bf16)
            down = (down.astype(f32) + last_down.astype(f32)).astype(bf16)
        return up, down

    def step(self, sends=None):
        parts, before = self.held
        n = len(before)
        up, down = sends or self.ready()
        self.held = parts, before + ((hop(up, 1, 0, n), hop(down, -1, 3 - n, 3)),)

    def total(self):
        parts, before = self.held
        up, down = before[-1]
        return parts[0].astype(f32) + up.astype(f32) + down.astype(f32)


def chunk_kernel(
    low, place_ref, wide_ref, long_ref, first_ref, mine_ref, other_ref, *rest
):
    summed = len(rest) > 1
    high = low + wide_ref.shape[1]
    half = mine_ref.shape[0]
    step = 256

    def mm(a, b):
        return lax.dot_general(a, b, (((1,), (1,)), ((), ())), preferred_element_type=f32)

    if summed:
        gain_ref, shift_ref, normed_ref, out_ref, sums_ref = rest

        @pl.when(pl.program_id(0) == 0)
        def _():
            sums_ref[...] = jnp.zeros_like(sums_ref)

    else:
        out_ref = rest[0]
    for c, weight_ref in enumerate((mine_ref, other_ref)):
        at = pl.ds(pl.multiple_of((place_ref[8] ^ c) * half, half), half)
        for start in range(0, wide_ref.shape[0], step):
            rows = slice(start, start + step)
            part = mm(wide_ref[rows, :], first_ref[at, low:high])
            part += mm(long_ref[rows, :], weight_ref[...])
            out_ref[0, rows, at] = part.astype(bf16)
            if summed:
                scaled = part * gain_ref[0, :, at].astype(f32)
                offset = normed_ref[rows, at].astype(f32) - shift_ref[0, :, at].astype(f32)
                sums_ref[0, rows, :] += jnp.sum(scaled, -1, keepdims=True)
                sums_ref[1, rows, :] += jnp.sum(part * offset, -1, keepdims=True)


def feature_chunks(place, wide, long, first, low, weight, norms=None):
    mine, other = weight
    rows = wide.shape[0]
    size = first.shape[0] // 4
    half = size // 2

    def resident(value):
        return pl.BlockSpec(value.shape, lambda i, p: (0, 0))

    def by_slot(value):
        return pl.BlockSpec((half, value.shape[1]), lambda i, p: (p[4 + i], 0))

    in_specs = [
        resident(wide),
        resident(long),
        pl.BlockSpec((size, first.shape[1]), lambda i, p: (p[i], 0)),
        by_slot(mine),
        by_slot(other),
    ]
    args = [wide, long, first, mine, other]
    out_specs = [pl.BlockSpec((1, rows, size), lambda i, p: (i, 0, 0))]
    out_shape = [jax.ShapeDtypeStruct((4, rows, size), bf16)]
    if norms is not None:
        gains, shifts, normed = norms
        line = pl.BlockSpec((1, 1, size), lambda i, p: (3 - i, 0, 0))
        in_specs += [line, line, pl.BlockSpec((rows, size), lambda i, p: (0, p[i]))]
        args += [gains[:, None, :], shifts[:, None, :], normed]
        out_specs += [pl.BlockSpec((2, rows, 1), lambda i, p: (0, 0, 0))]
        out_shape += [jax.ShapeDtypeStruct((2, rows, 1), f32)]
    out = pl.pallas_call(
        functools.partial(chunk_kernel, low),
        grid_spec=pltpu.PrefetchScalarGridSpec(
            num_scalar_prefetch=1, grid=(4,), in_specs=in_specs, out_specs=out_specs
        ),
        out_shape=out_shape,
        compiler_params=pltpu.CompilerParams(vmem_limit_bytes=VMEM),
        cost_estimate=SHORT,
    )(place, *args)
    return out if norms is not None else out[0]


def forward_kernel(rows_ref, mine_ref, other_ref, bias_ref, act_ref, slope_ref):
    half = mine_ref.shape[0]
    step = 256
    for start in range(0, rows_ref.shape[0], step):
        at = slice(start, start + step)
        h = jnp.dot(rows_ref[at, :half], mine_ref[...], preferred_element_type=f32)
        h += jnp.dot(rows_ref[at, half:], other_ref[...], preferred_element_type=f32)
        act, slope = gelu_and_slope(h + bias_ref[...].astype(f32))
        act_ref[at, :] = act.astype(bf16)
        slope_ref[at, :] = slope.astype(bf16)


def backward_kernel(rows_ref, mine_ref, other_ref, slope_ref, grad_ref, sum_ref):
    half = mine_ref.shape[0]
    step = 256
    total = jnp.zeros(sum_ref.shape, f32)
    for start in range(0, rows_ref.shape[0], step):
        at = slice(start, start + step)
        h = jnp.dot(rows_ref[at, :half], mine_ref[...], preferred_element_type=f32)
        h += jnp.dot(rows_ref[at, half:], other_ref[...], preferred_element_type=f32)
        h *= slope_ref[at, :].astype(f32)
        grad_ref[at, :] = h.astype(bf16)
        total += jnp.sum(h, axis=0, keepdims=True)
    sum_ref[...] = total


def hidden_layer(kernel, rows, weight, last, outs):
    mine, other = weight
    count, depth = rows.shape
    cols = mine.shape[1]
    tile = COLUMNS

    def spec(height):
        return pl.BlockSpec((height, tile), lambda i: (0, i))

    return pl.pallas_call(
        kernel,
        grid=(cols // tile,),
        in_specs=[
            pl.BlockSpec((count, depth), lambda i: (0, 0)),
            spec(depth // 2),
            spec(depth // 2),
            spec(last.shape[0]),
        ],
        out_specs=[spec(o.shape[0]) for o in outs],
        out_shape=outs,
        compiler_params=pltpu.CompilerParams(vmem_limit_bytes=VMEM),
        cost_estimate=SHORT,
    )(rows, mine, other, last)


def rotary_tables(length, lanes):
    half_rot = ROT // 2
    freqs = jnp.exp(jnp.arange(half_rot, dtype=f32) * (-2.0 * math.log(10000.0) / ROT))
    angles = jnp.arange(length, dtype=jnp.int32).astype(f32)[:, None] * freqs[None, :]
    cosine = jnp.cos(angles)
    sine = jnp.sin(angles)
    zero = jnp.zeros((length, half_rot), f32)
    rest_one = jnp.ones((length, HD - ROT), f32)
    rest_zero = jnp.zeros((length, HD - ROT), f32)
    keep = jnp.concatenate([cosine, cosine, rest_one], -1)
    from_high = jnp.concatenate([-sine, zero, rest_zero], -1)
    from_low = jnp.concatenate([zero, sine, rest_zero], -1)
    many = lanes // HD
    return jnp.stack([jnp.tile(v, (1, many)) for v in (keep, from_high, from_low)])


def attention_kernel(
    tile, slot_ref, q_ref, k_ref, v_ref, grad_ref, table_ref, attn_ref, dproj_ref, bias_ref, *scratch
):
    q_s, k_s, v_s, g_s, qt_s, kt_s, vt_s, gt_s, at_s, dqt_s, dk_s, dv_s = scratch
    length, lanes = q_ref.shape
    blocks = slot_ref.shape[0]
    block = length // blocks
    tiles = length // tile
    half_rot = ROT // 2
    scale = HD ** (-0.5)
    many = lanes // HD
    width = dproj_ref.shape[1] // 3

    def turn(u, at, sign):
        keep, high, low = table_ref[0, at, :], table_ref[1, at, :], table_ref[2, at, :]
        moved = pltpu.roll(u, lanes - half_rot, 1) * high + pltpu.roll(u, half_rot, 1) * low
        return u * keep + sign * moved

    def places(b):
        at = slice(b * block, (b + 1) * block)
        return at, pl.ds(pl.multiple_of(slot_ref[b] * block, block), block)

    for b in range(blocks):
        at, came = places(b)
        q = turn(q_ref[came, :], at, 1.0).astype(bf16).astype(f32) * scale
        k = turn(k_ref[came, :], at, 1.0).astype(bf16).astype(f32)
        v = v_ref[came, :].astype(bf16).astype(f32)
        g = grad_ref[came, :].astype(f32)
        for value, flat, turned in ((q, q_s, qt_s), (k, k_s, kt_s), (v, v_s, vt_s), (g, g_s, gt_s)):
            turned[:, at] = value.T.astype(bf16)
            for h in range(many):
                flat[h, at, :] = value[:, h * HD : (h + 1) * HD].astype(bf16)

    row = lax.broadcasted_iota(jnp.int32, (tile, tile), 0)
    col = lax.broadcasted_iota(jnp.int32, (tile, tile), 1)
    hidden = row > col

    def mm(a, b):
        return jnp.dot(a, b, preferred_element_type=f32)

    for h in range(many):
        feats = slice(h * HD, (h + 1) * HD)
        for i in range(tiles):
            qs = slice(i * tile, (i + 1) * tile)
            q_t = qt_s[feats, qs]
            scores = []
            for j in range(i + 1):
                s = mm(k_s[h, j * tile : (j + 1) * tile, :], q_t)
                scores.append(jnp.where(hidden, NEG_BIG, s) if j == i else s)
            top = functools.reduce(
                jnp.maximum, [jnp.max(s, axis=0, keepdims=True) for s in scores]
            )
            weights = [jnp.exp(s - top) for s in scores]
            total = functools.reduce(
                jnp.add, [jnp.sum(w, axis=0, keepdims=True) for w in weights]
            )
            mixed = functools.reduce(
                jnp.add,
                [
                    mm(vt_s[feats, j * tile : (j + 1) * tile], w.astype(bf16))
                    for j, w in enumerate(weights)
                ],
            )
            mixed = (mixed / total).astype(bf16).astype(f32)
            at_s[feats, qs] = mixed
            g_t = gt_s[feats, qs]
            delta = jnp.sum(g_t.astype(f32) * mixed, axis=0, keepdims=True)
            inverse = 1.0 / total
            dq = None
            for j in range(i + 1):
                ks = slice(j * tile, (j + 1) * tile)
                p = weights[j] * inverse
                dp = mm(v_s[h, ks, :], g_t)
                ds = (p * (dp - delta)).astype(bf16)
                dv = mm(p.astype(bf16), g_s[h, qs, :])
                dk = mm(ds, q_s[h, qs, :])
                if i == j:
                    dv_s[h, ks, :] = dv
                    dk_s[h, ks, :] = dk
                else:
                    dv_s[h, ks, :] += dv
                    dk_s[h, ks, :] += dk
                part = mm(kt_s[feats, ks], ds)
                dq = part if dq is None else dq + part
            dqt_s[feats, qs] = dq * scale

    sums = [jnp.zeros((1, lanes), f32) for _ in range(3)]
    for b in range(blocks):
        at, came = places(b)
        attn_ref[came, :] = at_s[:, at].T.astype(bf16)
        dq = turn(dqt_s[:, at].T, at, -1.0)
        dk = turn(jnp.concatenate([dk_s[h, at, :] for h in range(many)], 1), at, -1.0)
        dv = jnp.concatenate([dv_s[h, at, :] for h in range(many)], 1)
        for index, value in enumerate((dq, dk, dv)):
            lane = pl.multiple_of(index * width + pl.program_id(1) * lanes, lanes)
            dproj_ref[came, pl.ds(lane, lanes)] = value.astype(bf16)
            sums[index] = sums[index] + jnp.sum(value, axis=0, keepdims=True)
    for index in range(3):
        bias_ref[0, index] = sums[index]


def attention_whole(proj, attn_grad, plan, tables):
    rows = proj.shape[0]
    width = proj.shape[1] // 3
    per, members = plan.per, plan.members
    length = rows // per
    tile = min(256, length)
    many = LANES // HD
    steps = width // LANES
    slots = jnp.sum(
        jnp.where(
            plan.order[None, :] == jnp.arange(members, dtype=jnp.int32)[:, None],
            jnp.arange(members, dtype=jnp.int32)[None, :],
            0,
        ),
        axis=1,
    ).astype(jnp.int32)
    flat = pltpu.VMEM((many, length, HD), bf16)
    turned = pltpu.VMEM((LANES, length), bf16)
    wide = pltpu.VMEM((LANES, length), f32)
    sums = pltpu.VMEM((many, length, HD), f32)

    def columns(part):
        return pl.BlockSpec((length, LANES), lambda s, h, o: (s, part * steps + h))

    attn, dproj, bias = pl.pallas_call(
        functools.partial(attention_kernel, tile),
        grid_spec=pltpu.PrefetchScalarGridSpec(
            num_scalar_prefetch=1,
            grid=(per, steps),
            in_specs=[
                columns(0),
                columns(1),
                columns(2),
                columns(0),
                pl.BlockSpec((3, length, LANES), lambda s, h, o: (0, 0, 0)),
            ],
            out_specs=[
                columns(0),
                pl.BlockSpec((length, 3 * width), lambda s, h, o: (s, 0)),
                pl.BlockSpec((1, 3, 1, LANES), lambda s, h, o: (s, 0, 0, h)),
            ],
            scratch_shapes=[flat] * 4 + [turned] * 4 + [wide] * 2 + [sums] * 2,
        ),
        out_shape=[
            jax.ShapeDtypeStruct((rows, width), bf16),
            jax.ShapeDtypeStruct((rows, 3 * width), bf16),
            jax.ShapeDtypeStruct((per, 3, 1, width), f32),
        ],
        compiler_params=pltpu.CompilerParams(vmem_limit_bytes=VMEM),
        cost_estimate=SHORT,
    )(slots, proj, proj, proj, attn_grad, tables)
    return attn, dproj, jnp.sum(bias, axis=(0, 2)).reshape(-1)


def rotate(values, cosine, sine):
    half_rot = ROT // 2
    front = values[..., :ROT]
    turned = jnp.concatenate([-front[..., half_rot:], front[..., :half_rot]], -1)
    return jnp.concatenate([front * cosine + turned * sine, values[..., ROT:]], -1)


def rotate_back(grads, cosine, sine):
    half_rot = ROT // 2
    front = grads[..., :ROT]
    by_sine = front * sine
    turned = jnp.concatenate([by_sine[..., half_rot:], -by_sine[..., :half_rot]], -1)
    return jnp.concatenate([front * cosine + turned, grads[..., ROT:]], -1)


def attention_split(proj, attn_grad, plan, block_len):
    rows = attn_grad.shape[0]
    width = attn_grad.shape[1]
    per, members, groups = plan.per, plan.members, plan.groups
    count = rows // per
    heads = width // HD

    def positions(blocks):
        inside = jnp.arange(block_len, dtype=jnp.int32)
        return (blocks[:, None] * block_len + inside[None, :]).reshape(-1)

    position = positions(plan.order)
    every = positions(plan.all_order)
    half_rot = ROT // 2
    freqs = jnp.exp(jnp.arange(half_rot, dtype=f32) * (-2.0 * math.log(10000.0) / ROT))
    angles = position.astype(f32)[:, None] * freqs[None, :]
    cosine = jnp.concatenate([jnp.cos(angles)] * 2, -1)[None, :, None, :]
    sine = jnp.concatenate([jnp.sin(angles)] * 2, -1)[None, :, None, :]
    teams = [[m + members * g for g in range(groups)] for m in range(members)]

    def team_gather(value, axis):
        return lax.all_gather(
            value, "context", axis=axis, tiled=True, axis_index_groups=teams
        )

    def team_sum(value):
        return lax.psum_scatter(
            value, "context", scatter_dimension=1, tiled=True, axis_index_groups=teams
        )

    shape = (per, count, heads, HD)
    q = rotate(proj[:, :width].reshape(shape), cosine, sine).astype(bf16)
    k = rotate(proj[:, width : 2 * width].reshape(shape), cosine, sine).astype(bf16)
    v = proj[:, 2 * width :].reshape(shape).astype(bf16)
    g = attn_grad.reshape(shape)
    k_all = team_gather(k, 1)
    v_all = team_gather(v, 1)
    visible = every[None, :] <= position[:, None]
    scale = HD ** (-0.5)
    outs, dqs, dks, dvs = [], [], [], []
    for h in range(heads):
        s = dot("sqd,skd->sqk", q[:, :, h], k_all[:, :, h]) * scale
        s = jnp.where(visible, s, NEG_BIG)
        top = jnp.max(s, -1, keepdims=True)
        e = jnp.where(visible, jnp.exp(s - top), 0.0)
        total = jnp.sum(e, -1, keepdims=True)
        o = (dot("sqk,skd->sqd", e.astype(bf16), v_all[:, :, h]) / total).astype(bf16)
        delta = jnp.sum(g[:, :, h].astype(f32) * o.astype(f32), -1, keepdims=True)
        p = e / total
        dp = dot("sqd,skd->sqk", g[:, :, h], v_all[:, :, h])
        ds = (p * (dp - delta) * scale).astype(bf16)
        outs.append(o)
        dqs.append(dot("sqk,skd->sqd", ds, k_all[:, :, h]))
        dks.append(dot("sqk,sqd->skd", ds, q[:, :, h]))
        dvs.append(dot("sqk,sqd->skd", p.astype(bf16), g[:, :, h]))
    attn = jnp.concatenate(outs, -1).reshape(rows, width)
    dq = rotate_back(jnp.stack(dqs, 2), cosine, sine).reshape(rows, width)
    dk = team_sum(jnp.concatenate(dks, -1)).reshape(shape)
    dk = rotate_back(dk, cosine, sine).reshape(rows, width)
    dv = team_sum(jnp.concatenate(dvs, -1)).reshape(rows, width)
    dproj = jnp.concatenate([dq, dk, dv], -1)
    return attn, dproj.astype(bf16), jnp.sum(dproj, axis=0)


def general_block(
    block_in,
    norm_gain,
    layer_norm_bias,
    qkv_weight,
    qkv_bias,
    out_weight,
    out_bias,
    fc1_weight,
    fc1_bias,
    fc2_weight,
    fc2_bias,
    block_order,
    out_grad,
):
    seq_count, block_len, width = block_in.shape
    plan = Rows(seq_count, block_order)
    x_own = plan.gather(block_in)
    g_own = plan.gather(out_grad)
    qkv_flat = qkv_weight.swapaxes(0, 1).reshape(qkv_weight.shape[1], -1)
    qkv_full = lax.all_gather(qkv_flat, "context", axis=0, tiled=True)
    out_full = lax.all_gather(out_weight, "context", axis=1, tiled=True)
    fc1_full = lax.all_gather(fc1_weight, "context", axis=0, tiled=True)
    fc2_full = lax.all_gather(fc2_weight, "context", axis=1, tiled=True)
    x_full, g_full, gain, shift = (
        lax.all_gather(v, "tensor", axis=v.ndim - 1, tiled=True)
        for v in (x_own, g_own, norm_gain, layer_norm_bias)
    )
    centred = x_full.astype(f32)
    mean = jnp.mean(centred, -1, keepdims=True)
    centred = centred - mean
    inv_std = lax.rsqrt(jnp.mean(centred * centred, -1, keepdims=True) + NORM_EPS)
    xhat = centred * inv_std
    normed = (xhat * gain.astype(f32) + shift.astype(f32)).astype(bf16)

    proj = dot("rd,de->re", normed, qkv_full) + qkv_bias.astype(f32).reshape(-1)
    attn_grad = dot("rd,ed->re", g_full, out_full).astype(bf16)
    if plan.groups == 1:
        tables = rotary_tables(proj.shape[0] // plan.per, LANES)
        attn, dproj, qkvb_sum = attention_whole(proj, attn_grad, plan, tables)
    else:
        attn, dproj, qkvb_sum = attention_split(proj, attn_grad, plan, block_len)
    hidden_pre = dot("rd,df->rf", normed, fc1_full) + fc1_bias.astype(f32)
    hidden_act, slope = gelu_and_slope(hidden_pre)
    hidden_act = hidden_act.astype(bf16)
    hidden_grad = dot("rd,fd->rf", g_full, fc2_full) * slope
    fc1b_sum = jnp.sum(hidden_grad, axis=0)
    hidden_grad = hidden_grad.astype(bf16)

    def rows_summed(part):
        part = part.astype(bf16)
        return lax.psum_scatter(part, "context", scatter_dimension=0, tiled=True).astype(f32)

    qkv_w_g = rows_summed(dot("rd,re->de", normed, dproj))
    out_w_g = rows_summed(dot("rd,re->de", g_full, attn))
    fc2_w_g = rows_summed(dot("rd,rf->df", g_full, hidden_act))
    fc1_w_g = rows_summed(dot("rd,rf->df", normed, hidden_grad))

    def features_summed(value):
        value = value.astype(bf16)
        return lax.psum_scatter(value, "tensor", scatter_dimension=1, tiled=True).astype(f32)

    part = dot("re,de->rd", dproj, qkv_full) + dot("rf,df->rd", hidden_grad, fc1_full)
    scaled = part * gain.astype(f32)
    row_sums = jnp.stack([jnp.sum(scaled, -1), jnp.sum(scaled * xhat, -1)])
    row_sums = sum_over(row_sums, "tensor")
    norm_own = features_summed(part)
    branch = features_summed(
        dot("re,ed->rd", attn, out_full) + dot("rf,fd->rd", hidden_act, fc2_full)
    )
    change, sums = row_change(x_own, mean, inv_std, row_sums, norm_own, norm_gain)
    return finish(
        (block_in, out_grad, out_bias, fc2_bias, qkv_bias),
        (plan.scatter(change), plan.scatter(branch.astype(bf16))),
        (qkvb_sum, jnp.sum(out_grad.astype(f32), axis=(0, 1)), fc1b_sum, *sums),
        (jnp.concatenate([qkv_w_g, out_w_g], 1), 3 * width, fc1_w_g, fc2_w_g),
    )


def row_change(x_own, mean, inv_std, row_sums, norm_own, norm_gain):
    xhat_own = (x_own.astype(f32) - mean) * inv_std
    row_means = row_sums / (x_own.shape[1] * lax.axis_size("tensor"))
    change = inv_std * (
        norm_own * norm_gain.astype(f32)
        - row_means[0][:, None]
        - xhat_own * row_means[1][:, None]
    )
    sums = jnp.sum(norm_own * xhat_own, axis=0), jnp.sum(norm_own, axis=0)
    return change.astype(bf16), sums


def finish(given, rows, bias_sums, weights):
    block_in, out_grad, out_bias, fc2_bias, qkv_bias = given
    change, branch = rows
    qkvb_sum, outb_sum, fc1b_sum, gain_sum, beta_sum = bias_sums
    attn_w_g, qkv_width, fc1_w_g, fc2_w_g = weights
    width = block_in.shape[-1]
    block_out = (
        block_in.astype(f32)
        + branch.astype(f32)
        + out_bias.astype(f32)
        + fc2_bias.astype(f32)
    ).astype(bf16)
    grad_own = out_grad.astype(f32)
    input_grad = grad_own + change.astype(f32)

    sums = (qkvb_sum, outb_sum, fc1b_sum, gain_sum, beta_sum)
    joined = sum_over(jnp.concatenate(sums), "context")
    cuts = []
    start = 0
    for part in sums:
        cuts.append(joined[start : start + part.shape[0]])
        start += part.shape[0]
    qkv_b_g, outb_g, fc1_b_g, gain_g, beta_g = cuts
    return (
        block_out,
        input_grad,
        gain_g,
        beta_g,
        attn_w_g[:, :qkv_width].reshape(-1, 3, width).swapaxes(0, 1),
        qkv_b_g.reshape(qkv_bias.shape),
        attn_w_g[:, qkv_width:].T,
        outb_g,
        fc1_w_g,
        fc1_b_g,
        fc2_w_g.T,
        outb_g,
    )


def staged_block(
    block_in,
    norm_gain,
    layer_norm_bias,
    qkv_weight,
    qkv_bias,
    out_weight,
    out_bias,
    fc1_weight,
    fc1_bias,
    fc2_weight,
    fc2_bias,
    block_order,
    out_grad,
):
    seq_count, block_len, width = block_in.shape
    plan = Rows(seq_count, block_order)
    ctx = lax.axis_index("context")
    z, k = ctx // 2, ctx % 2
    ten = lax.axis_index("tensor")
    qkv_width = 3 * width

    norm_pieces = neighbours(jnp.stack([norm_gain, layer_norm_bias]))
    x_own = plan.gather(block_in)
    first = jnp.concatenate(
        [qkv_weight.swapaxes(0, 1).reshape(qkv_weight.shape[1], -1), out_weight.T], 1
    )
    fc2_own = fc2_weight.T
    tables = rotary_tables(plan.members * block_len, LANES)
    outb_sum = jnp.sum(out_grad.astype(f32), axis=(0, 1))
    x_own, norm_pieces, first, fc2_own, grad_in, tables, outb_sum = fence(
        x_own, norm_pieces, first, fc2_own, out_grad, tables, outb_sum
    )
    first_full = lax.all_gather(first, "context", axis=0, tiled=True)
    g_own = plan.gather(grad_in)
    near = [swap(x_own, "tensor", m) for m in (1, 2)]
    spread = Spread(fc1_weight, fc2_own)
    x_pieces, g_own, spread.own = fence(far_pieces(x_own, near), g_own, spread.own)
    spread.step()
    near = [swap(g_own, "tensor", m) for m in (1, 2)]
    gains = jnp.stack([p[0] for p in norm_pieces])
    shifts = jnp.stack([p[1] for p in norm_pieces])
    g_pieces = far_pieces(g_own, near)
    normed, normed_c, normed_t, normed_o, mean, inv_std = join_features(
        x_pieces, gains, shifts
    )
    g_full, g_c, g_t, g_o = join_features(g_pieces)
    first_full, normed, normed_c, normed_t, normed_o, g_full, g_c, g_t, g_o = fence(
        first_full, normed, normed_c, normed_t, normed_o, g_full, g_c, g_t, g_o
    )
    first_full, spread.got = fence(first_full, spread.got)
    qkv_full = first_full[:, :qkv_width]
    out_full = first_full[:, qkv_width:]

    spread.step()
    normed_o, g_o = swap(normed_o, "context", 1), swap(g_o, "context", 1)
    proj = dot("rd,de->re", normed, qkv_full) + qkv_bias.astype(f32).reshape(-1)
    attn_grad = dot("rd,de->re", g_full, out_full).astype(bf16)
    attn, dproj, qkvb_sum = attention_whole(proj, attn_grad, plan, tables)
    spread.got, attn, dproj, normed_o, g_o = fence(spread.got, attn, dproj, normed_o, g_o)

    spread.step()
    attn_sum = ChainSum(
        (normed_t, dproj, normed_o, swap(dproj, "context", 1)),
        (g_t, attn, g_o, swap(attn, "context", 1)),
    )
    (attn_sum.held,) = fence(attn_sum.held)

    attn_sum.step()
    spread.got, attn_sum.held = fence(spread.got, attn_sum.held)

    fc1_mine, sends = fence(spread.joined(0), attn_sum.ready())
    attn_sum.step(sends)
    fc1_full = fc1_mine, swap(fc1_mine, "context", 1)
    (fc1_full,) = fence(fc1_full)

    wide = jax.ShapeDtypeStruct((normed_c.shape[0], fc1_bias.shape[0]), bf16)
    hidden_act, slope = hidden_layer(
        forward_kernel, normed_c, fc1_full, fc1_bias.reshape(1, -1), [wide, wide]
    )
    spread.got, hidden_act, slope, attn_sum.held = fence(
        spread.got, hidden_act, slope, attn_sum.held
    )

    hidden_o = swap(hidden_act, "context", 1)
    fc2_mine, hidden_o, sends = fence(spread.joined(1), hidden_o, attn_sum.ready())
    attn_sum.step(sends)
    fc2_full = fc2_mine, swap(fc2_mine, "context", 1)
    fc2_sum = ChainSum((g_t, hidden_act, g_o, hidden_o))
    fc2_full, fc2_sum.held, attn_sum.held = fence(fc2_full, fc2_sum.held, attn_sum.held)

    fc2_sum.step()
    line = jax.ShapeDtypeStruct((1, fc1_bias.shape[0]), f32)
    hidden_grad, fc1b_sum = hidden_layer(
        backward_kernel, g_c, fc2_full, slope, [wide, line]
    )
    fc1b_sum = fc1b_sum.reshape(-1)
    fc2_sum.held, hidden_grad, attn = fence(fc2_sum.held, hidden_grad, attn)

    masks = jnp.arange(3, -1, -1, dtype=jnp.int32)
    owners = ten.astype(jnp.int32) ^ masks
    place = jnp.concatenate([owners, (z - owners) & 3, k.reshape(1)]).astype(jnp.int32)
    fc2_sum.step()
    hidden_grad_o = swap(hidden_grad, "context", 1)
    chunks = feature_chunks(place, attn, hidden_act, first_full, qkv_width, fc2_full)
    fc2_sum.held, hidden_grad_o, chunks = fence(fc2_sum.held, hidden_grad_o, chunks)

    fc2_sum.step()
    branch_sum = FeatureSum(chunks)
    fc1_sum = ChainSum((normed_t, hidden_grad, normed_o, hidden_grad_o))
    fc2_sum.held, branch_sum.held, fc1_sum.held, dproj = fence(
        fc2_sum.held, branch_sum.held, fc1_sum.held, dproj
    )

    fc1_sum.step()
    branch_sum.step()
    norm_chunks, row_sums = feature_chunks(
        place, dproj, hidden_grad, first_full, 0, fc1_full, (gains, shifts, normed)
    )
    fc1_sum.held, branch_sum.held, norm_chunks, row_sums = fence(
        fc1_sum.held, branch_sum.held, norm_chunks, row_sums
    )

    sends = fc1_sum.ready()
    branch = branch_sum.total().astype(bf16)
    sends, branch, norm_chunks, row_sums = fence(sends, branch, norm_chunks, row_sums)
    fc1_sum.step(sends)
    norm_sum = FeatureSum(norm_chunks)
    branch = plan.scatter(branch)
    row_sums = sum(neighbours(row_sums[..., 0]))
    attn_w_g = attn_sum.total()
    norm_sum.held, row_sums, attn_w_g = fence(norm_sum.held, row_sums, attn_w_g)
    norm_sum.step()
    fc2_w_g = fc2_sum.total()
    fc1_sum.held, norm_sum.held, fc2_w_g = fence(fc1_sum.held, norm_sum.held, fc2_w_g)

    sends = fc1_sum.ready()
    change, sums = row_change(x_own, mean, inv_std, row_sums, norm_sum.total(), norm_gain)
    sends, change, branch = fence(sends, change, branch)
    fc1_sum.step(sends)
    change = plan.scatter(change)
    return finish(
        (block_in, out_grad, out_bias, fc2_bias, qkv_bias),
        (change, branch),
        (qkvb_sum, outb_sum, fc1b_sum, *sums),
        (attn_w_g, qkv_width, fc1_sum.total(), fc2_w_g),
    )


def on_device(*args):
    block_in, block_order = args[0], args[11]
    four = lax.axis_size("context") == 8 and lax.axis_size("tensor") == 4
    if four and block_in.shape[0] % 8 == 0:
        return staged_block(*args)
    return general_block(*args)


def solution(mesh):
    rows = P(None, "context", "tensor")
    in_specs = (
        rows,
        P("tensor"),
        P("tensor"),
        P(None, "context", "tensor"),
        P(None, "tensor"),
        P("tensor", "context"),
        P("tensor"),
        P("context", "tensor"),
        P("tensor"),
        P("tensor", "context"),
        P("tensor"),
        P(),
        rows,
    )
    out_specs = (
        rows,
        rows,
        P("tensor"),
        P("tensor"),
        P(None, "context", "tensor"),
        P(None, "tensor"),
        P("tensor", "context"),
        P("tensor"),
        P("context", "tensor"),
        P("tensor"),
        P("tensor", "context"),
        P("tensor"),
    )
    return jax.shard_map(
        on_device, mesh=mesh, in_specs=in_specs, out_specs=out_specs, check_vma=False
    )
```
